1024 devices in a mesh: dp: 128 (over x, z, core), tensor: 8 (over y).
Axes of the slice: x: 4, y: 8, z: 16, core: 2. Of those that a mesh axis runs over, the one named last changes fastest.
Arguments:
- q_ctx: bfloat16 [16384, 4096], P('dp', 'tensor'), may hold values from -0.119628906 to 0.119628906
- p_ctx: bfloat16 [2048, 4096], P('dp', 'tensor'), may hold values from -0.119628906 to 0.119628906
- out_weight: bfloat16 [4096, 4096], P('tensor'), may hold values from -0.09375 to 0.09375
- neighbours: int32 [128, 8], P('dp'), may hold values from 0 to 127, as said below
- positive: int32 [16384], P('dp'), may hold values from 0 to 127
Outputs:
- q_grad: bfloat16 [16384, 4096], P('dp', 'tensor')
- p_grad: bfloat16 [2048, 4096], P('dp', 'tensor')
- losses: float32 [16384], P('dp')
The draws below stay inside these ranges and needn't reach their ends.
Inputs may be any that keep to these rules, and one draw needn't show every extreme that they name: `neighbours`: row i lists 8 different blocks: first i itself, then blocks (i + o) mod 128 with 1 <= o <= 14; some row lists the block at distance 14.
All inputs are finite; a program needn't handle non-finite values.
Results may differ from the reference program's by a relative error of at most 0.012.
Values may be sent and summed in bfloat16 or wider, within the bound.
No kernel may reach another device: no remote copies, remote signals or barrier semaphores. Data moves between devices by JAX's collectives and lax.ppermute only.
A program may use at most 32 MiB of HBM per device.

```python
import jax
import jax.numpy as jnp
from jax import lax

D = 4096
H = 4096
QD = 128
PD = 16
NBR = 8
NQ = 16384
NP = 2048
REACH = 14
N_DP = 128


def draw_neighbours(key, part):
    key = jax.random.fold_in(key, 7)
    row_keys = jax.random.split(jax.random.fold_in(key, 1), N_DP)

    def one_row(row_key):
        return jax.random.permutation(row_key, REACH).astype(jnp.int32) + 1
    perms = jax.vmap(one_row)(row_keys)
    chosen = jax.random.randint(jax.random.fold_in(key, 2), (), 0, N_DP).astype(jnp.int32)
    columns = jnp.arange(REACH, dtype=jnp.int32)[None, :]
    where_far = jnp.sum(jnp.where(perms == REACH, columns, 0), axis=1, keepdims=True).astype(jnp.int32)
    last_taken = perms[:, NBR - 2:NBR - 1]
    moved = jnp.where(columns == where_far, last_taken, perms)
    moved = jnp.where(columns == NBR - 2, REACH, moved)
    rows = jnp.arange(N_DP, dtype=jnp.int32)[:, None]
    perms = jnp.where(rows == chosen, moved, perms)
    offsets = jnp.concatenate([jnp.zeros((N_DP, 1), jnp.int32), perms[:, :NBR - 1]], axis=1)
    return ((rows + offsets) % N_DP).astype(jnp.int32)


def touch_ends(drawn, own_key, least, largest):
    shape = drawn.shape
    spot = [jax.random.randint(jax.random.fold_in(own_key, axis), (), 0, shape[axis]) for axis in range(len(shape))]
    drawn = drawn.at[tuple(spot)].set(least)
    longest = shape.index(max(shape))
    spot[longest] = (spot[longest] + 1) % shape[longest]
    return drawn.at[tuple(spot)].set(largest)


def levels(key, shape, shards, low, top_value):
    def one(position, shards_of):
        heights = jax.random.uniform(jax.random.fold_in(jax.random.fold_in(key, 6), position), (shards_of,), jnp.float32, low / len(shards), top_value / len(shards))
        return jnp.repeat(jnp.exp(heights), shape[position] // shards_of).reshape((-1,) + (1,) * (len(shape) - position - 1))

    loudness = one(*shards[0])
    for cut in shards[1:]:
        loudness = loudness * one(*cut)
    return loudness


def bell_draw(rng, dims, width, most, cuts=(), kind=jnp.bfloat16):
    level = levels(rng, dims, cuts, -0.22, 0.18) if cuts else 1.0
    result = jax.random.normal(rng, dims, jnp.float32) * width * level
    return jnp.minimum(jnp.maximum(result, -most), most).astype(kind)


def setup_inputs(seed: int = 0) -> dict:
    streams_of = jax.random.split(jax.random.key(seed), 6)
    return {
        "q_ctx": bell_draw(streams_of[0], (NQ, H), 0.02, 0.119628906, ((0, 128), (1, 8))),
        "p_ctx": bell_draw(streams_of[1], (NP, H), 0.02, 0.119628906, ((0, 128), (1, 8))),
        "out_weight": bell_draw(streams_of[2], (H, D), H ** -0.5, 0.09375, ((0, 8),)),
        "neighbours": draw_neighbours(jax.random.fold_in(streams_of[5], 71), 0),
        "positive": touch_ends(jax.random.randint(streams_of[4], (NQ,), 0, NBR * PD), jax.random.fold_in(streams_of[4], 1), 0, (NBR * PD) - 1).astype(jnp.int32),
    }


SCALE = 50.0
EPS = 1e-06

def embed(ctx, out_weight):
    pre = jnp.dot(ctx, out_weight, preferred_element_type=jnp.float32)
    norm = jnp.sqrt(lax.optimization_barrier(jnp.sum(pre * pre, axis=-1, keepdims=True)) + EPS)
    return (pre / norm, norm)

def reference(q_ctx, p_ctx, out_weight, neighbours, positive):
    ctx = jnp.concatenate([q_ctx, p_ctx], axis=0)
    emb, norm = embed(ctx, out_weight)
    emb_b = emb.astype(jnp.bfloat16)
    q_emb = emb_b[:NQ].reshape(N_DP, QD, D)
    p_blocks = emb_b[NQ:].reshape(N_DP, PD, D)
    slots = jnp.arange(NBR * PD, dtype=jnp.int32)

    def per_block(items):
        q_block, listed, pos = items
        cand = p_blocks[listed].reshape(NBR * PD, D)
        scores = jnp.dot(q_block, cand.T, preferred_element_type=jnp.float32) * SCALE
        lse = jnp.log(lax.optimization_barrier(jnp.sum(jnp.exp(scores), axis=-1)))
        onehot = (slots[None, :] == pos[:, None]).astype(jnp.float32)
        loss = lse - lax.optimization_barrier(jnp.sum(scores * onehot, axis=-1))
        dscore = (jnp.exp(scores - lse[:, None]) - onehot).astype(jnp.bfloat16)
        dq = jnp.dot(dscore, cand, preferred_element_type=jnp.float32) * SCALE
        dcand = jnp.dot(dscore.T, q_block, preferred_element_type=jnp.float32) * SCALE
        return (loss, dq, dcand.reshape(NBR, PD, D))
    losses, dq, dcand = lax.map(per_block, (q_emb, neighbours, positive.reshape(N_DP, QD)))
    dpass = jnp.zeros((N_DP, PD, D), jnp.float32).at[neighbours].add(dcand)
    demb = jnp.concatenate([dq.reshape(NQ, D), dpass.reshape(NP, D)], axis=0).astype(jnp.bfloat16)
    demb_f = demb.astype(jnp.float32)
    inner = lax.optimization_barrier(jnp.sum(emb * demb_f, axis=-1, keepdims=True))
    dpre = ((demb_f - emb * inner) / norm).astype(jnp.bfloat16)
    grads = jnp.dot(dpre, out_weight.T, preferred_element_type=jnp.float32).astype(jnp.bfloat16)
    return (grads[:NQ], grads[NQ:], losses.reshape(NQ))
```

```python
import jax
import jax.numpy as jnp
from jax import lax
from jax.sharding import Mesh
from jax.sharding import PartitionSpec as P

SCALE = 50.0
EPS = 1e-06
WINDOW = 8
CORES = 2
MEMBERS = ("core", "tensor")
CHIPS = ("w", "zlo")


def shift_chips(value, by):
    chips = lax.axis_size(CHIPS)
    return lax.ppermute(value, CHIPS, [(i, (i + by) % chips) for i in range(chips)])


def halves(value, parts):
    out = []
    for _ in range(parts):
        top = lax.reduce_precision(value, 8, 7)
        out.append(top.astype(jnp.bfloat16))
        value = value - top
    return out


def on_device(q_ctx, p_ctx, out_weight, neighbours, positive):
    f32, bf16 = jnp.float32, jnp.bfloat16
    q_rows, p_rows = q_ctx.shape[0], p_ctx.shape[0]
    listed = neighbours.shape[1]
    slots = listed * p_rows
    tensors = lax.axis_size("tensor")
    members = CORES * tensors
    feats = out_weight.shape[1] // members
    q_part = q_rows // tensors
    core, place = lax.axis_index("core"), lax.axis_index("zlo")

    far_ctx = shift_chips(p_ctx, -WINDOW)
    other = lax.ppermute(neighbours, "core", [(0, 1), (1, 0)])
    lists = jnp.concatenate([neighbours, other], axis=0)
    lists = jnp.where(core == 0, lists, lists[::-1])

    def project(rows):
        part = jnp.dot(rows, out_weight, preferred_element_type=f32).astype(bf16)
        return part.reshape(rows.shape[0], members, feats).transpose(1, 0, 2)

    def reduce_over_tensor(part):
        got = lax.all_to_all(part, MEMBERS, 0, 0)
        got = got.reshape(CORES, tensors, part.shape[1], feats).astype(f32)
        return jnp.sum(got, axis=1).astype(bf16)

    p_pre = reduce_over_tensor(project(jnp.concatenate([p_ctx, far_ctx], axis=0)))
    q_pre = reduce_over_tensor(project(q_ctx))
    near, far = p_pre[:, :p_rows], p_pre[:, p_rows:]

    ids = jnp.arange(WINDOW, dtype=jnp.int32)
    outgoing = jnp.where((ids <= place)[:, None, None, None], near[None], far[None])
    window = lax.all_to_all(outgoing, "zlo", 0, 0).reshape(WINDOW * CORES, p_rows, feats)
    spots = lists % (WINDOW * CORES)
    cand = window[spots].reshape(CORES, slots, feats)

    raw = jnp.einsum("kqf,kcf->kqc", q_pre, cand, preferred_element_type=f32)
    q_sq = jnp.sum(jnp.square(q_pre.astype(f32)), axis=-1)
    c_sq = jnp.sum(jnp.square(cand.astype(f32)), axis=-1)
    q_sq = jnp.pad(q_sq.reshape(CORES, tensors, 1, q_part), ((0, 0), (0, 0), (0, 0), (0, slots - q_part)))
    c_sq = jnp.broadcast_to(c_sq[:, None, None, :], (CORES, tensors, 1, slots))
    extra = jnp.zeros((CORES, tensors, 6, slots), f32)
    sums = jnp.concatenate([raw.reshape(CORES, tensors, q_part, slots), q_sq, c_sq, extra], axis=2)
    sums = lax.all_to_all(sums.reshape(members, q_part + 8, slots), MEMBERS, 0, 0)
    sums = jnp.sum(sums, axis=0)
    raw = sums[:q_part]
    inv_q = lax.rsqrt(sums[q_part, :q_part] + EPS)
    inv_c = lax.rsqrt(sums[q_part + 1] + EPS)

    scores = raw * (SCALE * inv_q)[:, None] * inv_c[None, :]
    lse = jnp.log(jnp.sum(jnp.exp(scores), axis=-1))
    pos = lax.dynamic_slice_in_dim(positive, lax.axis_index("tensor") * q_part, q_part)
    onehot = (jnp.arange(slots, dtype=jnp.int32)[None, :] == pos[:, None]).astype(f32)
    loss = lse - jnp.sum(scores * onehot, axis=-1)
    dscore = jnp.exp(scores - lse[:, None]) - onehot
    coef = lax.reduce_precision(dscore * (SCALE * inv_q)[:, None] * inv_c[None, :], 8, 7)
    weighted = coef * raw
    q_inner = jnp.square(inv_q) * jnp.sum(weighted, axis=-1)
    c_inner = jnp.square(inv_c) * jnp.sum(weighted, axis=0)

    row = jnp.concatenate(halves(q_inner, 2) + halves(loss, 3))
    row = jnp.pad(row, (0, slots - row.shape[0]))
    c_rows = jnp.stack([row] + halves(c_inner, 2) + [jnp.zeros((slots,), bf16)] * 5)
    told = jnp.concatenate([coef.astype(bf16), c_rows], axis=0)
    told = lax.all_to_all(jnp.broadcast_to(told[None], (members,) + told.shape), MEMBERS, 0, 0)
    told = told.reshape(CORES, tensors, q_part + 8, slots)
    coef = told[:, :, :q_part].reshape(CORES, q_rows, slots)
    row = told[:, :, q_part].astype(f32)
    q_inner = (row[..., :q_part] + row[..., q_part : 2 * q_part]).reshape(CORES, q_rows, 1)
    loss = row[..., 2 * q_part : 3 * q_part] + row[..., 3 * q_part : 4 * q_part] + row[..., 4 * q_part : 5 * q_part]
    losses = jnp.where(core == 0, loss[0], loss[1]).reshape(q_rows)
    c_inner = jnp.sum(told[:, :, q_part + 1 : q_part + 3].astype(f32), axis=(1, 2))[..., None]

    dq = jnp.einsum("kqc,kcf->kqf", coef, cand, preferred_element_type=f32)
    dq = (dq - q_inner * q_pre.astype(f32)).astype(bf16)
    dc = jnp.einsum("kqc,kqf->kcf", coef, q_pre, preferred_element_type=f32)
    dc = (dc - c_inner * cand.astype(f32)).astype(bf16)
    match = (jnp.arange(WINDOW * CORES, dtype=jnp.int32)[:, None, None] == spots[None]).astype(bf16)
    dwin = jnp.einsum("wks,kspf->wpf", match, dc.reshape(CORES, listed, p_rows, feats), preferred_element_type=f32)

    back = lax.all_to_all(dwin.astype(bf16).reshape(WINDOW, CORES, p_rows, feats), "zlo", 0, 0).astype(f32)
    mine = (ids <= place)[:, None, None, None]
    near = jnp.sum(jnp.where(mine, back, 0.0), axis=0)
    far = jnp.sum(jnp.where(mine, 0.0, back), axis=0).astype(bf16)
    dp = (near + shift_chips(far, WINDOW).astype(f32)).astype(bf16)

    def gather_features(part):
        part = jnp.broadcast_to(part[:, None], (CORES, tensors) + part.shape[1:])
        return lax.all_to_all(part.reshape((members,) + part.shape[2:]), MEMBERS, 0, 0)

    def unproject(part):
        weight = out_weight.reshape(out_weight.shape[0], members, feats)
        return jnp.einsum("mrf,hmf->rh", part, weight, preferred_element_type=f32).astype(bf16)

    q_grad = unproject(gather_features(dq))
    p_grad = unproject(gather_features(dp))
    return q_grad, p_grad, losses


def solution(mesh):
    dp, tensors = mesh.shape["dp"], mesh.shape["tensor"]
    fine = Mesh(
        mesh.devices.reshape(dp // (WINDOW * CORES), WINDOW, CORES, tensors), ("w", "zlo", "core", "tensor")
    )
    rows = ("w", "zlo", "core")
    placed = (P(rows, "tensor"), P(rows, "tensor"), P("tensor", None), P(rows, None), P(rows))
    return jax.shard_map(
        on_device,
        mesh=fine,
        in_specs=placed,
        out_specs=(P(rows, "tensor"), P(rows, "tensor"), P(rows)),
        check_vma=False,
    )
```

```python
import jax
import jax.numpy as jnp
from jax import lax
from jax.sharding import Mesh
from jax.sharding import PartitionSpec as P

SCALE = 50.0
EPS = 1e-06
WINDOW = 8
CORES = 2
MEMBERS = ("core", "tensor")


def shift_chips(value, by):
    chips = lax.axis_size("chip")
    return lax.ppermute(value, "chip", [(i, (i + by) % chips) for i in range(chips)])


def halves(value, parts):
    out = []
    for _ in range(parts):
        top = lax.reduce_precision(value, 8, 7)
        out.append(top.astype(jnp.bfloat16))
        value = value - top
    return out


def on_device(q_ctx, p_ctx, out_weight, neighbours, positive):
    f32, bf16 = jnp.float32, jnp.bfloat16
    q_rows, p_rows = q_ctx.shape[0], p_ctx.shape[0]
    listed = neighbours.shape[1]
    slots = listed * p_rows
    tensors = lax.axis_size("tensor")
    members = CORES * tensors
    feats = out_weight.shape[1] // members
    q_part = q_rows // tensors
    core, chip = lax.axis_index("core"), lax.axis_index("chip")

    other = lax.ppermute(neighbours, "core", [(0, 1), (1, 0)])
    lists = jnp.concatenate([neighbours, other], axis=0)
    lists = jnp.where(core == 0, lists, lists[::-1])

    def project(rows):
        part = jnp.dot(rows, out_weight, preferred_element_type=f32).astype(bf16)
        return part.reshape(rows.shape[0], members, feats).transpose(1, 0, 2)

    def reduce_over_tensor(part):
        got = lax.all_to_all(part, MEMBERS, 0, 0)
        got = got.reshape(CORES, tensors, part.shape[1], feats).astype(f32)
        return jnp.sum(got, axis=1).astype(bf16)

    p_part = project(p_ctx)
    q_ctx, p_part = lax.optimization_barrier((q_ctx, p_part))
    window = reduce_over_tensor(p_part)
    q_pre = reduce_over_tensor(project(q_ctx))

    reach = 1
    while reach < WINDOW:
        window = jnp.concatenate([window, shift_chips(window, -reach)], axis=0)
        reach *= 2
    spots = (lists - CORES * chip) % (CORES * lax.axis_size("chip"))
    cand = window[spots].reshape(CORES, slots, feats)

    raw = jnp.einsum("kqf,kcf->kqc", q_pre, cand, preferred_element_type=f32)
    q_sq = jnp.sum(jnp.square(q_pre.astype(f32)), axis=-1)
    c_sq = jnp.sum(jnp.square(cand.astype(f32)), axis=-1)
    q_sq = jnp.pad(q_sq.reshape(CORES, tensors, 1, q_part), ((0, 0), (0, 0), (0, 0), (0, slots - q_part)))
    c_sq = jnp.broadcast_to(c_sq[:, None, None, :], (CORES, tensors, 1, slots))
    extra = jnp.zeros((CORES, tensors, 6, slots), f32)
    sums = jnp.concatenate([raw.reshape(CORES, tensors, q_part, slots), q_sq, c_sq, extra], axis=2)
    sums = lax.all_to_all(sums.reshape(members, q_part + 8, slots), MEMBERS, 0, 0)
    sums = jnp.sum(sums, axis=0)
    raw = sums[:q_part]
    inv_q = lax.rsqrt(sums[q_part, :q_part] + EPS)
    inv_c = lax.rsqrt(sums[q_part + 1] + EPS)

    scores = raw * (SCALE * inv_q)[:, None] * inv_c[None, :]
    lse = jnp.log(jnp.sum(jnp.exp(scores), axis=-1))
    pos = lax.dynamic_slice_in_dim(positive, lax.axis_index("tensor") * q_part, q_part)
    onehot = (jnp.arange(slots, dtype=jnp.int32)[None, :] == pos[:, None]).astype(f32)
    loss = lse - jnp.sum(scores * onehot, axis=-1)
    dscore = jnp.exp(scores - lse[:, None]) - onehot
    coef = lax.reduce_precision(dscore * (SCALE * inv_q)[:, None] * inv_c[None, :], 8, 7)
    weighted = coef * raw
    q_inner = jnp.square(inv_q) * jnp.sum(weighted, axis=-1)
    c_inner = jnp.square(inv_c) * jnp.sum(weighted, axis=0)

    row = jnp.concatenate(halves(q_inner, 2) + halves(loss, 3))
    row = jnp.pad(row, (0, slots - row.shape[0]))
    c_rows = jnp.stack([row] + halves(c_inner, 2) + [jnp.zeros((slots,), bf16)] * 5)
    told = jnp.concatenate([coef.astype(bf16), c_rows], axis=0)
    told = lax.all_to_all(jnp.broadcast_to(told[None], (members,) + told.shape), MEMBERS, 0, 0)
    told = told.reshape(CORES, tensors, q_part + 8, slots)
    coef = told[:, :, :q_part].reshape(CORES, q_rows, slots)
    row = told[:, :, q_part].astype(f32)
    q_inner = (row[..., :q_part] + row[..., q_part : 2 * q_part]).reshape(CORES, q_rows, 1)
    loss = row[..., 2 * q_part : 3 * q_part] + row[..., 3 * q_part : 4 * q_part] + row[..., 4 * q_part : 5 * q_part]
    losses = jnp.where(core == 0, loss[0], loss[1]).reshape(q_rows)
    c_inner = jnp.sum(told[:, :, q_part + 1 : q_part + 3].astype(f32), axis=(1, 2))[..., None]

    dq = jnp.einsum("kqc,kcf->kqf", coef, cand, preferred_element_type=f32)
    dq = (dq - q_inner * q_pre.astype(f32)).astype(bf16)
    dc = jnp.einsum("kqc,kqf->kcf", coef, q_pre, preferred_element_type=f32)
    dc = (dc - c_inner * cand.astype(f32)).astype(bf16)
    match = (jnp.arange(WINDOW * CORES, dtype=jnp.int32)[:, None, None] == spots[None]).astype(bf16)
    dwin = jnp.einsum("wks,kspf->wpf", match, dc.reshape(CORES, listed, p_rows, feats), preferred_element_type=f32)

    while reach > 1:
        reach //= 2
        away = shift_chips(dwin[CORES * reach :].astype(bf16), reach)
        dwin = dwin[: CORES * reach] + away.astype(f32)
    dp = dwin.astype(bf16)

    def gather_features(part):
        part = jnp.broadcast_to(part[:, None], (CORES, tensors) + part.shape[1:])
        return lax.all_to_all(part.reshape((members,) + part.shape[2:]), MEMBERS, 0, 0)

    def unproject(part):
        weight = out_weight.reshape(out_weight.shape[0], members, feats)
        return jnp.einsum("mrf,hmf->rh", part, weight, preferred_element_type=f32).astype(bf16)

    q_all = gather_features(dq)
    q_all, dp = lax.optimization_barrier((q_all, dp))
    p_grad = unproject(gather_features(dp))
    return unproject(q_all), p_grad, losses


def solution(mesh):
    dp, tensors = mesh.shape["dp"], mesh.shape["tensor"]
    fine = Mesh(mesh.devices.reshape(dp // CORES, CORES, tensors), ("chip", "core", "tensor"))
    rows = ("chip", "core")
    placed = (P(rows, "tensor"), P(rows, "tensor"), P("tensor", None), P(rows, None), P(rows))
    return jax.shard_map(
        on_device,
        mesh=fine,
        in_specs=placed,
        out_specs=(P(rows, "tensor"), P(rows, "tensor"), P(rows)),
        check_vma=False,
    )
```

```python
import jax
import jax.numpy as jnp
from jax import lax
from jax.sharding import Mesh
from jax.sharding import PartitionSpec as P

SCALE = 50.0
EPS = 1e-06
WINDOW = 8
CORES = 2
TENSOR = ("u", "par")
MEMBERS = ("core",) + TENSOR
ALIKE = ("core", "u")


def shift_chips(value, by):
    chips = lax.axis_size("chip")
    return lax.ppermute(value, "chip", [(i, (i + by) % chips) for i in range(chips)])


def swap(value, odd):
    peers = lax.axis_size(TENSOR)
    return lax.ppermute(value, TENSOR, [(t, (t + (1 if t % 2 == odd else -1)) % peers) for t in range(peers)])


def halves(value, parts):
    out = []
    for _ in range(parts):
        top = lax.reduce_precision(value, 8, 7)
        out.append(top.astype(jnp.bfloat16))
        value = value - top
    return out


def on_device(q_ctx, p_ctx, out_weight, neighbours, positive):
    f32, bf16 = jnp.float32, jnp.bfloat16
    q_rows, p_rows = q_ctx.shape[0], p_ctx.shape[0]
    listed = neighbours.shape[1]
    slots = listed * p_rows
    tensors = lax.axis_size(TENSOR)
    members = CORES * tensors
    feats = out_weight.shape[1] // members
    q_share = q_rows // tensors
    core, chip = lax.axis_index("core"), lax.axis_index("chip")

    other = lax.ppermute(neighbours, "core", [(0, 1), (1, 0)])
    lists = jnp.concatenate([neighbours, other], axis=0)
    lists = jnp.where(core == 0, lists, lists[::-1])

    def project(rows):
        part = jnp.dot(rows, out_weight, preferred_element_type=f32).astype(bf16)
        return part.reshape(rows.shape[0], members, feats).transpose(1, 0, 2)

    def reduce_over_tensor(part):
        got = lax.all_to_all(part, MEMBERS, 0, 0)
        got = got.reshape(CORES, tensors, part.shape[1], feats).astype(f32)
        return jnp.sum(got, axis=1).astype(bf16)

    p_part = project(p_ctx)
    q_ctx, p_part = lax.optimization_barrier((q_ctx, p_part))
    window = reduce_over_tensor(p_part)
    parity = lax.axis_index("par")
    q_part = project(q_ctx).reshape(CORES, tensors // 2, 2, q_rows, feats)
    keep = jnp.where(parity == 0, q_part[:, :, 0], q_part[:, :, 1])
    send = jnp.where(parity == 0, q_part[:, :, 1], q_part[:, :, 0])
    got = jnp.stack([swap(send[0], 0), swap(send[1], 1)])
    q_pair = (keep.astype(f32) + got.astype(f32)).astype(bf16)
    q_pair = lax.all_to_all(q_pair.reshape(members // 2, q_rows, feats), ALIKE, 0, 0)
    q_pre = jnp.sum(q_pair.reshape(CORES, tensors // 2, q_rows, feats).astype(f32), axis=1).astype(bf16)

    window = jnp.concatenate([window] + [shift_chips(window, -by) for by in range(1, WINDOW // 2)], axis=0)
    window = jnp.concatenate([window, shift_chips(window, -(WINDOW // 2))], axis=0)
    spots = (lists - CORES * chip) % (CORES * lax.axis_size("chip"))
    cand = window[spots].reshape(CORES, slots, feats)

    raw = jnp.einsum("kqf,kcf->kqc", q_pre, cand, preferred_element_type=f32)
    q_sq = jnp.sum(jnp.square(q_pre.astype(f32)), axis=-1)
    c_sq = jnp.sum(jnp.square(cand.astype(f32)), axis=-1)
    q_sq = jnp.pad(q_sq.reshape(CORES, tensors, 1, q_share), ((0, 0), (0, 0), (0, 0), (0, slots - q_share)))
    c_sq = jnp.broadcast_to(c_sq[:, None, None, :], (CORES, tensors, 1, slots))
    extra = jnp.zeros((CORES, tensors, 6, slots), f32)
    sums = jnp.concatenate([raw.reshape(CORES, tensors, q_share, slots), q_sq, c_sq, extra], axis=2)
    sums = lax.all_to_all(sums.reshape(members, q_share + 8, slots), MEMBERS, 0, 0)
    sums = jnp.sum(sums, axis=0)
    raw = sums[:q_share]
    inv_q = lax.rsqrt(sums[q_share, :q_share] + EPS)
    inv_c = lax.rsqrt(sums[q_share + 1] + EPS)

    scores = raw * (SCALE * inv_q)[:, None] * inv_c[None, :]
    lse = jnp.log(jnp.sum(jnp.exp(scores), axis=-1))
    pos = lax.dynamic_slice_in_dim(positive, lax.axis_index(TENSOR) * q_share, q_share)
    onehot = (jnp.arange(slots, dtype=jnp.int32)[None, :] == pos[:, None]).astype(f32)
    loss = lse - jnp.sum(scores * onehot, axis=-1)
    dscore = jnp.exp(scores - lse[:, None]) - onehot
    coef = lax.reduce_precision(dscore * (SCALE * inv_q)[:, None] * inv_c[None, :], 8, 7)
    weighted = coef * raw
    q_inner = jnp.square(inv_q) * jnp.sum(weighted, axis=-1)
    c_inner = jnp.square(inv_c) * jnp.sum(weighted, axis=0)

    row = jnp.concatenate(halves(q_inner, 2) + halves(loss, 3))
    row = jnp.pad(row, (0, slots - row.shape[0]))
    c_rows = jnp.stack([row] + halves(c_inner, 2) + [jnp.zeros((slots,), bf16)] * 5)
    told = jnp.concatenate([coef.astype(bf16), c_rows], axis=0)
    told = lax.all_to_all(jnp.broadcast_to(told[None], (members,) + told.shape), MEMBERS, 0, 0)
    told = told.reshape(CORES, tensors, q_share + 8, slots)
    coef = told[:, :, :q_share].reshape(CORES, q_rows, slots)
    row = told[:, :, q_share].astype(f32)
    q_inner = (row[..., :q_share] + row[..., q_share : 2 * q_share]).reshape(CORES, q_rows, 1)
    loss = row[..., 2 * q_share : 3 * q_share] + row[..., 3 * q_share : 4 * q_share] + row[..., 4 * q_share : 5 * q_share]
    losses = jnp.where(core == 0, loss[0], loss[1]).reshape(q_rows)
    c_inner = jnp.sum(told[:, :, q_share + 1 : q_share + 3].astype(f32), axis=(1, 2))[..., None]

    dq = jnp.einsum("kqc,kcf->kqf", coef, cand, preferred_element_type=f32)
    dq = (dq - q_inner * q_pre.astype(f32)).astype(bf16)
    dc = jnp.einsum("kqc,kqf->kcf", coef, q_pre, preferred_element_type=f32)
    dc = (dc - c_inner * cand.astype(f32)).astype(bf16)
    match = (jnp.arange(WINDOW * CORES, dtype=jnp.int32)[:, None, None] == spots[None]).astype(bf16)
    dwin = jnp.einsum("wks,kspf->wpf", match, dc.reshape(CORES, listed, p_rows, feats), preferred_element_type=f32)

    half = dwin.shape[0] // 2
    dwin = dwin[:half] + shift_chips(dwin[half:].astype(bf16), WINDOW // 2).astype(f32)
    dwin = dwin.reshape(WINDOW // 2, CORES, p_rows, feats)
    away = [shift_chips(dwin[by].astype(bf16), by) for by in range(1, WINDOW // 2)]
    dp = sum([part.astype(f32) for part in away], dwin[0]).astype(bf16)

    def unproject(part):
        weight = out_weight.reshape(out_weight.shape[0], members, feats)
        return jnp.einsum("mrf,hmf->rh", part, weight, preferred_element_type=f32).astype(bf16)

    dq = jnp.broadcast_to(dq[:, None], (CORES, tensors // 2, q_rows, feats))
    dq = lax.all_to_all(dq.reshape(members // 2, q_rows, feats), ALIKE, 0, 0)
    dq, dp = lax.optimization_barrier((dq, dp))
    dp = jnp.broadcast_to(dp[:, None], (CORES, tensors, p_rows, feats))
    dp = lax.all_to_all(dp.reshape(members, p_rows, feats), MEMBERS, 0, 0)
    dq = dq.reshape(CORES, tensors // 2, q_rows, feats)
    got = jnp.stack([swap(dq[0], 0), swap(dq[1], 1)])
    dq = jnp.where(parity == 0, jnp.stack([dq, got], axis=2), jnp.stack([got, dq], axis=2))
    q_grad = unproject(dq.reshape(members, q_rows, feats))
    return q_grad, unproject(dp), losses


def solution(mesh):
    dp, tensors = mesh.shape["dp"], mesh.shape["tensor"]
    fine = Mesh(mesh.devices.reshape(dp // CORES, CORES, tensors // 2, 2), ("chip",) + MEMBERS)
    rows = ("chip", "core")
    placed = (P(rows, TENSOR), P(rows, TENSOR), P(TENSOR, None), P(rows, None), P(rows))
    return jax.shard_map(
        on_device,
        mesh=fine,
        in_specs=placed,
        out_specs=(P(rows, TENSOR), P(rows, TENSOR), P(rows)),
        check_vma=False,
    )
```

```python
import jax
import jax.numpy as jnp
from jax import lax
from jax.experimental import pallas as pl
from jax.experimental.pallas import tpu as pltpu
from jax.sharding import Mesh
from jax.sharding import PartitionSpec as P

SCALE = 50.0
EPS = 1e-06
WINDOW = 8
CORES = 2
MEMBERS = ("core", "tensor")
STEPS = 4
NT = (((1,), (1,)), ((), ()))


def shift_chips(value, by):
    chips = lax.axis_size("chip")
    return lax.ppermute(value, "chip", [(i, (i + by) % chips) for i in range(chips)])


def halves(value, parts):
    out = []
    for _ in range(parts):
        top = lax.reduce_precision(value, 8, 7)
        out.append(top.astype(jnp.bfloat16))
        value = value - top
    return out


def project_kernel(x_ref, w_ref, _, out_ref):
    per, _, feats = out_ref.shape
    for j in range(per):
        part = jnp.dot(x_ref[...], w_ref[:, j * feats : (j + 1) * feats], preferred_element_type=jnp.float32)
        out_ref[j] = part.astype(out_ref.dtype)


def project(rows, weight, members, wanted):
    (count, depth), width = rows.shape, weight.shape[1]
    per, feats = members // STEPS, width // members
    return pl.pallas_call(
        project_kernel,
        grid=(STEPS,),
        in_specs=[
            pl.BlockSpec((count, depth), lambda g: (0, 0)),
            pl.BlockSpec((depth, width // STEPS), lambda g: (0, g)),
            pl.BlockSpec(memory_space=pl.ANY),
        ],
        out_specs=pl.BlockSpec((per, count, feats), lambda g: (g, 0, 0)),
        out_shape=jax.ShapeDtypeStruct((members, count, feats), jnp.bfloat16),
        cost_estimate=pl.CostEstimate(
            flops=2 * count * depth * width, bytes_accessed=2 * depth * width, transcendentals=0
        ),
    )(rows, weight, wanted)


def unproject_kernel(x_ref, w_ref, out_ref, sum_ref):
    step = pl.program_id(0)
    per, feats = x_ref.shape[0] // STEPS, x_ref.shape[2]

    @pl.when(step == 0)
    def _():
        sum_ref[...] = jnp.zeros_like(sum_ref)

    total = sum_ref[...]
    for j in range(per):
        total += lax.dot_general(
            x_ref[step * per + j], w_ref[:, j * feats : (j + 1) * feats], NT, preferred_element_type=jnp.float32
        )
    sum_ref[...] = total

    @pl.when(step == STEPS - 1)
    def _():
        out_ref[...] = total.astype(out_ref.dtype)


def unproject(part, weight):
    _, rows, _ = part.shape
    depth, width = weight.shape
    return pl.pallas_call(
        unproject_kernel,
        grid=(STEPS,),
        in_specs=[
            pl.BlockSpec(memory_space=pltpu.VMEM),
            pl.BlockSpec((depth, width // STEPS), lambda g: (0, g)),
        ],
        out_specs=pl.BlockSpec((rows, depth), lambda g: (0, 0)),
        out_shape=jax.ShapeDtypeStruct((rows, depth), jnp.bfloat16),
        scratch_shapes=[pltpu.VMEM((rows, depth), jnp.float32)],
        cost_estimate=pl.CostEstimate(
            flops=2 * rows * depth * width, bytes_accessed=2 * depth * width, transcendentals=0
        ),
    )(part, weight)


def on_device(q_ctx, p_ctx, out_weight, neighbours, positive):
    f32, bf16 = jnp.float32, jnp.bfloat16
    q_rows, p_rows = q_ctx.shape[0], p_ctx.shape[0]
    listed = neighbours.shape[1]
    slots = listed * p_rows
    tensors = lax.axis_size("tensor")
    members = CORES * tensors
    feats = out_weight.shape[1] // members
    q_share = q_rows // tensors
    core, chip = lax.axis_index("core"), lax.axis_index("chip")

    other = lax.ppermute(neighbours, "core", [(0, 1), (1, 0)])
    lists = jnp.concatenate([neighbours, other], axis=0)
    lists = jnp.where(core == 0, lists, lists[::-1])

    def reduce_over_tensor(part):
        got = lax.all_to_all(part, MEMBERS, 0, 0)
        got = got.reshape(CORES, tensors, part.shape[1], feats).astype(f32)
        return jnp.sum(got, axis=1).astype(bf16)

    window = reduce_over_tensor(project(p_ctx, out_weight, members, neighbours))
    q_pre = reduce_over_tensor(project(q_ctx, out_weight, members, other))

    reach = WINDOW // 2
    while reach:
        window = jnp.concatenate([window, shift_chips(window, -reach)], axis=0)
        reach //= 2
    ahead = (lists - CORES * chip) % (CORES * lax.axis_size("chip"))
    places = jnp.array([0, 4, 2, 6, 1, 5, 3, 7], jnp.int32)
    spots = jnp.sum(jnp.where(ahead[..., None] // CORES == places, jnp.arange(WINDOW, dtype=jnp.int32), 0), axis=-1)
    spots = spots * CORES + ahead % CORES
    cand = window[spots].reshape(CORES, slots, feats)

    raw = jnp.einsum("kqf,kcf->kqc", q_pre, cand, preferred_element_type=f32)
    q_sq = jnp.sum(jnp.square(q_pre.astype(f32)), axis=-1)
    c_sq = jnp.sum(jnp.square(cand.astype(f32)), axis=-1)
    q_sq = jnp.pad(q_sq.reshape(CORES, tensors, 1, q_share), ((0, 0), (0, 0), (0, 0), (0, slots - q_share)))
    c_sq = jnp.broadcast_to(c_sq[:, None, None, :], (CORES, tensors, 1, slots))
    extra = jnp.zeros((CORES, tensors, 6, slots), f32)
    sums = jnp.concatenate([raw.reshape(CORES, tensors, q_share, slots), q_sq, c_sq, extra], axis=2)
    sums = lax.all_to_all(sums.reshape(members, q_share + 8, slots), MEMBERS, 0, 0)
    sums = jnp.sum(sums, axis=0)
    raw = sums[:q_share]
    inv_q = lax.rsqrt(sums[q_share, :q_share] + EPS)
    inv_c = lax.rsqrt(sums[q_share + 1] + EPS)

    scores = raw * (SCALE * inv_q)[:, None] * inv_c[None, :]
    lse = jnp.log(jnp.sum(jnp.exp(scores), axis=-1))
    pos = lax.dynamic_slice_in_dim(positive, lax.axis_index("tensor") * q_share, q_share)
    onehot = (jnp.arange(slots, dtype=jnp.int32)[None, :] == pos[:, None]).astype(f32)
    loss = lse - jnp.sum(scores * onehot, axis=-1)
    dscore = jnp.exp(scores - lse[:, None]) - onehot
    coef = lax.reduce_precision(dscore * (SCALE * inv_q)[:, None] * inv_c[None, :], 8, 7)
    weighted = coef * raw
    q_inner = jnp.square(inv_q) * jnp.sum(weighted, axis=-1)
    c_inner = jnp.square(inv_c) * jnp.sum(weighted, axis=0)

    row = jnp.concatenate(halves(q_inner, 2) + halves(loss, 3))
    row = jnp.pad(row, (0, slots - row.shape[0]))
    c_rows = jnp.stack([row] + halves(c_inner, 2) + [jnp.zeros((slots,), bf16)] * 5)
    told = jnp.concatenate([coef.astype(bf16), c_rows], axis=0)
    told = lax.all_to_all(jnp.broadcast_to(told[None], (members,) + told.shape), MEMBERS, 0, 0)
    told = told.reshape(CORES, tensors, q_share + 8, slots)
    coef = told[:, :, :q_share].reshape(CORES, q_rows, slots)
    row = told[:, :, q_share].astype(f32)
    q_inner = (row[..., :q_share] + row[..., q_share : 2 * q_share]).reshape(CORES, q_rows, 1)
    loss = row[..., 2 * q_share : 3 * q_share] + row[..., 3 * q_share : 4 * q_share] + row[..., 4 * q_share : 5 * q_share]
    losses = jnp.where(core == 0, loss[0], loss[1]).reshape(q_rows)
    c_inner = jnp.sum(told[:, :, q_share + 1 : q_share + 3].astype(f32), axis=(1, 2))[..., None]

    dq = jnp.einsum("kqc,kcf->kqf", coef, cand, preferred_element_type=f32)
    dq = (dq - q_inner * q_pre.astype(f32)).astype(bf16)
    dc = jnp.einsum("kqc,kqf->kcf", coef, q_pre, preferred_element_type=f32)
    dc = (dc - c_inner * cand.astype(f32)).astype(bf16)
    match = (jnp.arange(WINDOW * CORES, dtype=jnp.int32)[:, None, None] == spots[None]).astype(bf16)
    dwin = jnp.einsum("wks,kspf->wpf", match, dc.reshape(CORES, listed, p_rows, feats), preferred_element_type=f32)

    def gather_features(part):
        part = jnp.broadcast_to(part[:, None], (CORES, tensors) + part.shape[1:])
        return lax.all_to_all(part.reshape((members,) + part.shape[2:]), MEMBERS, 0, 0)

    dq = gather_features(dq)
    reach = 1
    while reach < WINDOW:
        half = dwin.shape[0] // 2
        dwin = dwin[:half] + shift_chips(dwin[half:].astype(bf16), reach).astype(f32)
        reach *= 2
    dp, dq = lax.optimization_barrier((dwin.astype(bf16), dq))

    return unproject(dq, out_weight), unproject(gather_features(dp), out_weight), losses


def solution(mesh):
    dp, tensors = mesh.shape["dp"], mesh.shape["tensor"]
    fine = Mesh(mesh.devices.reshape(dp // CORES, CORES, tensors), ("chip",) + MEMBERS)
    rows = ("chip", "core")
    placed = (P(rows, "tensor"), P(rows, "tensor"), P("tensor", None), P(rows, None), P(rows))
    return jax.shard_map(
        on_device,
        mesh=fine,
        in_specs=placed,
        out_specs=(P(rows, "tensor"), P(rows, "tensor"), P(rows)),
        check_vma=False,
    )
```

```python
import jax
import jax.numpy as jnp
from jax import lax
from jax.sharding import Mesh
from jax.sharding import PartitionSpec as P

SCALE = 50.0
EPS = 1e-06
WINDOW = 8
PLACES = (0, 4, 2, 6, 1, 5, 3, 7)
CORES = 2


def shift_chips(value, by):
    chips = lax.axis_size("chip")
    return lax.ppermute(value, "chip", [(i, (i + by) % chips) for i in range(chips)])


def swap_cores(value):
    return lax.ppermute(value, "core", [(0, 1), (1, 0)])


def halves(value, parts):
    out = []
    for _ in range(parts):
        top = lax.reduce_precision(value, 8, 7)
        out.append(top.astype(jnp.bfloat16))
        value = value - top
    return out


def on_device(q_ctx, p_ctx, out_weight, neighbours, positive):
    f32, bf16 = jnp.float32, jnp.bfloat16
    q_rows, p_rows = q_ctx.shape[0], p_ctx.shape[0]
    listed = neighbours.shape[1]
    slots = listed * p_rows
    tensors = lax.axis_size("tensor")
    feats = out_weight.shape[1] // tensors
    q_share = q_rows // tensors
    core, chip = lax.axis_index("core"), lax.axis_index("chip")

    ahead = (neighbours[0] - CORES * chip) % (CORES * lax.axis_size("chip"))
    spots = jnp.sum(
        jnp.where(ahead[:, None] // CORES == jnp.array(PLACES), jnp.arange(WINDOW, dtype=jnp.int32), 0), axis=-1
    )
    spots = spots + jnp.where(ahead % CORES == core, 0, WINDOW)

    def project(rows):
        part = jnp.dot(rows, out_weight, preferred_element_type=f32).astype(bf16)
        return part.reshape(rows.shape[0], tensors, feats).transpose(1, 0, 2)

    def exchange(part):
        return lax.all_to_all(part, "tensor", 0, 0)

    p_part = project(p_ctx)
    q_ctx, p_part = lax.optimization_barrier((q_ctx, p_part))
    window = jnp.sum(exchange(p_part).astype(f32), axis=0).astype(bf16)[None]
    q_pre = jnp.sum(exchange(project(q_ctx)).astype(f32), axis=0).astype(bf16)

    reach = WINDOW // 2
    while reach:
        window = jnp.concatenate([window, shift_chips(window, -reach)], axis=0)
        reach //= 2
    window = jnp.concatenate([window, swap_cores(window)], axis=0)
    cand = window[spots].reshape(slots, feats)

    whole = lax.all_gather(jnp.concatenate([q_pre, cand], axis=0), "tensor")
    weight = out_weight.reshape(out_weight.shape[0], tensors, feats)
    back = jnp.einsum("mrf,hmf->rh", whole, weight, preferred_element_type=f32)

    raw = jnp.dot(q_pre, cand.T, preferred_element_type=f32)
    q_sq = jnp.sum(jnp.square(q_pre.astype(f32)), axis=-1)
    c_sq = jnp.sum(jnp.square(cand.astype(f32)), axis=-1)
    q_sq = jnp.pad(q_sq.reshape(tensors, 1, q_share), ((0, 0), (0, 0), (0, slots - q_share)))
    c_sq = jnp.broadcast_to(c_sq[None, None, :], (tensors, 1, slots))
    extra = jnp.zeros((tensors, 6, slots), f32)
    sums = jnp.concatenate([raw.reshape(tensors, q_share, slots), q_sq, c_sq, extra], axis=1)
    sums = jnp.sum(exchange(sums), axis=0)
    raw = sums[:q_share]
    inv_q = lax.rsqrt(sums[q_share, :q_share] + EPS)
    inv_c = lax.rsqrt(sums[q_share + 1] + EPS)

    scores = raw * (SCALE * inv_q)[:, None] * inv_c[None, :]
    lse = jnp.log(jnp.sum(jnp.exp(scores), axis=-1))
    pos = lax.dynamic_slice_in_dim(positive, lax.axis_index("tensor") * q_share, q_share)
    onehot = (jnp.arange(slots, dtype=jnp.int32)[None, :] == pos[:, None]).astype(f32)
    loss = lse - jnp.sum(scores * onehot, axis=-1)
    dscore = jnp.exp(scores - lse[:, None]) - onehot
    coef = lax.reduce_precision(dscore * (SCALE * inv_q)[:, None] * inv_c[None, :], 8, 7)
    weighted = coef * raw
    q_inner = jnp.square(inv_q) * jnp.sum(weighted, axis=-1)
    c_inner = jnp.square(inv_c) * jnp.sum(weighted, axis=0)

    row = jnp.concatenate(halves(q_inner, 2) + halves(loss, 3))
    row = jnp.pad(row, (0, slots - row.shape[0]))
    c_rows = jnp.stack([row] + halves(c_inner, 2) + [jnp.zeros((slots,), bf16)] * 5)
    told = jnp.concatenate([coef.astype(bf16), c_rows], axis=0)
    told = exchange(jnp.broadcast_to(told[None], (tensors,) + told.shape))
    coef = told[:, :q_share].reshape(q_rows, slots)
    row = told[:, q_share].astype(f32)
    q_inner = (row[:, :q_share] + row[:, q_share : 2 * q_share]).reshape(q_rows, 1)
    losses = row[:, 2 * q_share : 3 * q_share] + row[:, 3 * q_share : 4 * q_share] + row[:, 4 * q_share : 5 * q_share]
    c_inner = jnp.sum(told[:, q_share + 1 : q_share + 3].astype(f32), axis=(0, 1))[:, None]

    dc = lax.dot_general(coef, q_pre, (((0,), (0,)), ((), ())), preferred_element_type=f32)
    dc = (dc - c_inner * cand.astype(f32)).astype(bf16).reshape(listed, p_rows * feats)
    match = (jnp.arange(CORES * WINDOW, dtype=jnp.int32)[:, None] == spots[None]).astype(bf16)
    dwin = jnp.dot(match, dc, preferred_element_type=f32).reshape(CORES * WINDOW, p_rows, feats)
    dwin = dwin[:WINDOW] + swap_cores(dwin[WINDOW:].astype(bf16)).astype(f32)
    reach = 1
    while reach < WINDOW:
        half = dwin.shape[0] // 2
        dwin = dwin[:half] + shift_chips(dwin[half:].astype(bf16), reach).astype(f32)
        reach *= 2
    dp = exchange(jnp.broadcast_to(dwin.astype(bf16), (tensors, p_rows, feats)))
    p_grad = jnp.einsum("mrf,hmf->rh", dp, weight, preferred_element_type=f32).astype(bf16)

    q_grad = jnp.dot(coef, back[q_rows:].astype(bf16), preferred_element_type=f32) - q_inner * back[:q_rows]
    return q_grad.astype(bf16), p_grad, losses.reshape(q_rows)


def solution(mesh):
    dp, tensors = mesh.shape["dp"], mesh.shape["tensor"]
    fine = Mesh(mesh.devices.reshape(dp // CORES, CORES, tensors), ("chip", "core", "tensor"))
    rows = ("chip", "core")
    placed = (P(rows, "tensor"), P(rows, "tensor"), P("tensor", None), P(rows, None), P(rows))
    return jax.shard_map(
        on_device,
        mesh=fine,
        in_specs=placed,
        out_specs=(P(rows, "tensor"), P(rows, "tensor"), P(rows)),
        check_vma=False,
    )
```

```python
import jax
import jax.numpy as jnp
from jax import lax
from jax.sharding import Mesh
from jax.sharding import PartitionSpec as P

SCALE = 50.0
EPS = 1e-06
WINDOW = 8
CORES = 2
MEMBERS = ("core", "tensor")


def shift_chips(value, by):
    chips = lax.axis_size("chip")
    return lax.ppermute(value, "chip", [(i, (i + by) % chips) for i in range(chips)])


def once(there, value):
    mark = there.ravel()[0]
    return jnp.where(mark == mark, value, jnp.zeros_like(value))


def halves(value, parts):
    out = []
    for _ in range(parts):
        top = lax.reduce_precision(value, 8, 7)
        out.append(top.astype(jnp.bfloat16))
        value = value - top
    return out


def on_device(q_ctx, p_ctx, out_weight, neighbours, positive):
    f32, bf16 = jnp.float32, jnp.bfloat16
    q_rows, p_rows = q_ctx.shape[0], p_ctx.shape[0]
    listed = neighbours.shape[1]
    slots = listed * p_rows
    tensors = lax.axis_size("tensor")
    members = CORES * tensors
    feats = out_weight.shape[1] // members
    q_part = q_rows // tensors
    core, chip = lax.axis_index("core"), lax.axis_index("chip")

    other = lax.ppermute(neighbours, "core", [(0, 1), (1, 0)])
    lists = jnp.concatenate([neighbours, other], axis=0)
    lists = jnp.where(core == 0, lists, lists[::-1])

    ahead = (lists - CORES * chip) % (CORES * lax.axis_size("chip"))
    far = ahead // CORES
    spots = (far % 2 * 4 + far // 2 % 2 * 2 + far // 4) * CORES + ahead % CORES

    def project(rows):
        part = jnp.dot(rows, out_weight, preferred_element_type=f32).astype(bf16)
        return part.reshape(rows.shape[0], members, feats).transpose(1, 0, 2)

    def reduce_over_tensor(part):
        got = lax.all_to_all(part, MEMBERS, 0, 0)
        got = got.reshape(CORES, tensors, part.shape[1], feats).astype(f32)
        return jnp.sum(got, axis=1).astype(bf16)

    p_part = project(p_ctx)
    q_ctx = once(spots.astype(f32), q_ctx)
    window = reduce_over_tensor(p_part)
    q_pre = reduce_over_tensor(project(q_ctx))

    reach = WINDOW // 2
    while reach:
        window = jnp.concatenate([window, shift_chips(window, -reach)], axis=0)
        reach //= 2
    cand = window[spots].reshape(CORES, slots, feats)

    raw = jnp.einsum("kqf,kcf->kqc", q_pre, cand, preferred_element_type=f32)
    q_sq = jnp.sum(jnp.square(q_pre.astype(f32)), axis=-1)
    c_sq = jnp.sum(jnp.square(cand.astype(f32)), axis=-1)
    q_sq = jnp.pad(q_sq.reshape(CORES, tensors, 1, q_part), ((0, 0), (0, 0), (0, 0), (0, slots - q_part)))
    c_sq = jnp.broadcast_to(c_sq[:, None, None, :], (CORES, tensors, 1, slots))
    extra = jnp.zeros((CORES, tensors, 6, slots), f32)
    sums = jnp.concatenate([raw.reshape(CORES, tensors, q_part, slots), q_sq, c_sq, extra], axis=2)
    sums = lax.all_to_all(sums.reshape(members, q_part + 8, slots), MEMBERS, 0, 0)
    sums = jnp.sum(sums, axis=0)
    raw = sums[:q_part]
    inv_q = lax.rsqrt(sums[q_part, :q_part] + EPS)
    inv_c = lax.rsqrt(sums[q_part + 1] + EPS)

    scores = raw * (SCALE * inv_q)[:, None] * inv_c[None, :]
    lse = jnp.log(jnp.sum(jnp.exp(scores), axis=-1))
    pos = lax.dynamic_slice_in_dim(positive, lax.axis_index("tensor") * q_part, q_part)
    onehot = (jnp.arange(slots, dtype=jnp.int32)[None, :] == pos[:, None]).astype(f32)
    loss = lse - jnp.sum(scores * onehot, axis=-1)
    dscore = jnp.exp(scores - lse[:, None]) - onehot
    coef = lax.reduce_precision(dscore * (SCALE * inv_q)[:, None] * inv_c[None, :], 8, 7)
    weighted = coef * raw
    q_inner = jnp.square(inv_q) * jnp.sum(weighted, axis=-1)
    c_inner = jnp.square(inv_c) * jnp.sum(weighted, axis=0)

    row = jnp.concatenate(halves(q_inner, 2) + halves(loss, 3))
    row = jnp.pad(row, (0, slots - row.shape[0]))
    c_rows = jnp.stack([row] + halves(c_inner, 2) + [jnp.zeros((slots,), bf16)] * 5)
    told = jnp.concatenate([coef.astype(bf16), c_rows], axis=0)
    told = lax.all_to_all(jnp.broadcast_to(told[None], (members,) + told.shape), MEMBERS, 0, 0)
    told = told.reshape(CORES, tensors, q_part + 8, slots)
    coef = told[:, :, :q_part].reshape(CORES, q_rows, slots)
    row = told[:, :, q_part].astype(f32)
    q_inner = (row[..., :q_part] + row[..., q_part : 2 * q_part]).reshape(CORES, q_rows, 1)
    loss = row[..., 2 * q_part : 3 * q_part] + row[..., 3 * q_part : 4 * q_part] + row[..., 4 * q_part : 5 * q_part]
    losses = jnp.where(core == 0, loss[0], loss[1]).reshape(q_rows)
    c_inner = jnp.sum(told[:, :, q_part + 1 : q_part + 3].astype(f32), axis=(1, 2))[..., None]

    dq = jnp.einsum("kqc,kcf->kqf", coef, cand, preferred_element_type=f32)
    dq = (dq - q_inner * q_pre.astype(f32)).astype(bf16)
    dc = jnp.einsum("kqc,kqf->kcf", coef, q_pre, preferred_element_type=f32)
    dc = (dc - c_inner * cand.astype(f32)).astype(bf16)
    match = (jnp.arange(WINDOW * CORES, dtype=jnp.int32)[:, None, None] == spots[None]).astype(bf16)
    dwin = jnp.einsum("wks,kspf->wpf", match, dc.reshape(CORES, listed, p_rows, feats), preferred_element_type=f32)

    reach = 1
    while reach < WINDOW:
        half = dwin.shape[0] // 2
        dwin = dwin[:half] + shift_chips(dwin[half:].astype(bf16), reach).astype(f32)
        reach *= 2
    dp = dwin.astype(bf16)

    def gather_features(part):
        part = jnp.broadcast_to(part[:, None], (CORES, tensors) + part.shape[1:])
        return lax.all_to_all(part.reshape((members,) + part.shape[2:]), MEMBERS, 0, 0)

    def unproject(part):
        weight = out_weight.reshape(out_weight.shape[0], members, feats)
        return jnp.einsum("mrf,hmf->rh", part, weight, preferred_element_type=f32).astype(bf16)

    q_all = gather_features(dq)
    q_all, dp = lax.optimization_barrier((q_all, dp))
    p_grad = unproject(gather_features(dp))
    return unproject(q_all), p_grad, losses


def solution(mesh):
    dp, tensors = mesh.shape["dp"], mesh.shape["tensor"]
    fine = Mesh(mesh.devices.reshape(dp // CORES, CORES, tensors), ("chip", "core", "tensor"))
    rows = ("chip", "core")
    placed = (P(rows, "tensor"), P(rows, "tensor"), P("tensor", None), P(rows, None), P(rows))
    return jax.shard_map(
        on_device,
        mesh=fine,
        in_specs=placed,
        out_specs=(P(rows, "tensor"), P(rows, "tensor"), P(rows)),
        check_vma=False,
    )
```

```python
import jax
import jax.numpy as jnp
from jax import lax
from jax.sharding import Mesh
from jax.sharding import PartitionSpec as P

SCALE = 50.0
EPS = 1e-06
WINDOW = 8
CORES = 2


def shift_chips(value, by):
    chips = lax.axis_size("chip")
    return lax.ppermute(value, "chip", [(i, (i + by) % chips) for i in range(chips)])


def swap_cores(value):
    return lax.ppermute(value, "core", [(0, 1), (1, 0)])


def on_device(q_ctx, p_ctx, out_weight, neighbours, positive):
    f32, bf16 = jnp.float32, jnp.bfloat16
    q_rows, p_rows = q_ctx.shape[0], p_ctx.shape[0]
    listed = neighbours.shape[1]
    slots = listed * p_rows
    tensors = lax.axis_size("tensor")
    feats = out_weight.shape[1] // tensors
    core, chip = lax.axis_index("core"), lax.axis_index("chip")

    ahead = (neighbours[0] - CORES * chip) % (CORES * lax.axis_size("chip"))
    spots = ahead // CORES + jnp.where(ahead % CORES == core, 0, WINDOW)

    def project(rows):
        part = jnp.dot(rows, out_weight, preferred_element_type=f32).astype(bf16)
        return part.reshape(rows.shape[0], tensors, feats).transpose(1, 0, 2)

    def exchange(part):
        return lax.all_to_all(part, "tensor", 0, 0)

    p_part = project(p_ctx)
    q_ctx, p_part = lax.optimization_barrier((q_ctx, p_part))
    window = jnp.sum(exchange(p_part).astype(f32), axis=0).astype(bf16)[None]
    q_pre = jnp.sum(exchange(project(q_ctx)).astype(f32), axis=0).astype(bf16)

    reach = 1
    while reach < WINDOW:
        window = jnp.concatenate([window, shift_chips(window, -reach)], axis=0)
        reach *= 2
    window = jnp.concatenate([window, swap_cores(window)], axis=0)
    cand = window[spots].reshape(slots, feats)

    raw = jnp.dot(q_pre, cand.T, preferred_element_type=f32)
    q_sq = jnp.sum(jnp.square(q_pre.astype(f32)), axis=-1)
    c_sq = jnp.sum(jnp.square(cand.astype(f32)), axis=-1)
    sums = jnp.concatenate([raw, q_sq.reshape(-1, slots), c_sq[None], jnp.zeros((7 - q_rows // slots, slots), f32)])
    sums = jnp.sum(exchange(jnp.broadcast_to(sums, (tensors,) + sums.shape)), axis=0)
    raw = sums[:q_rows]
    inv_q = lax.rsqrt(sums[q_rows : q_rows + q_rows // slots].reshape(q_rows) + EPS)
    inv_c = lax.rsqrt(sums[q_rows + q_rows // slots] + EPS)

    scores = raw * (SCALE * inv_q)[:, None] * inv_c[None, :]
    lse = jnp.log(jnp.sum(jnp.exp(scores), axis=-1))
    onehot = (jnp.arange(slots, dtype=jnp.int32)[None, :] == positive[:, None]).astype(f32)
    losses = lse - jnp.sum(scores * onehot, axis=-1)
    dscore = jnp.exp(scores - lse[:, None]) - onehot
    coef = lax.reduce_precision(dscore * (SCALE * inv_q)[:, None] * inv_c[None, :], 8, 7)
    weighted = coef * raw
    q_inner = (jnp.square(inv_q) * jnp.sum(weighted, axis=-1))[:, None]
    c_inner = (jnp.square(inv_c) * jnp.sum(weighted, axis=0))[:, None]
    coef = coef.astype(bf16)

    dq = jnp.dot(coef, cand, preferred_element_type=f32)
    dq = (dq - q_inner * q_pre.astype(f32)).astype(bf16)
    dq = exchange(jnp.broadcast_to(dq, (tensors,) + dq.shape))

    dc = lax.dot_general(coef, q_pre, (((0,), (0,)), ((), ())), preferred_element_type=f32)
    dc = (dc - c_inner * cand.astype(f32)).astype(bf16).reshape(listed, p_rows * feats)
    match = (jnp.arange(CORES * WINDOW, dtype=jnp.int32)[:, None] == spots[None]).astype(bf16)
    dwin = jnp.dot(match, dc, preferred_element_type=f32).reshape(CORES * WINDOW, p_rows, feats)
    dwin = dwin[:WINDOW] + swap_cores(dwin[WINDOW:].astype(bf16)).astype(f32)
    reach = WINDOW
    while reach > 1:
        reach //= 2
        dwin = dwin[:reach] + shift_chips(dwin[reach:].astype(bf16), reach).astype(f32)
    dp = dwin.astype(bf16)

    dq, dp = lax.optimization_barrier((dq, dp))
    dp = exchange(jnp.broadcast_to(dp, (tensors, p_rows, feats)))
    weight = out_weight.reshape(out_weight.shape[0], tensors, feats)

    def unproject(part):
        return jnp.einsum("mrf,hmf->rh", part, weight, preferred_element_type=f32).astype(bf16)

    return unproject(dq), unproject(dp), losses


def solution(mesh):
    dp, tensors = mesh.shape["dp"], mesh.shape["tensor"]
    fine = Mesh(mesh.devices.reshape(dp // CORES, CORES, tensors), ("chip", "core", "tensor"))
    rows = ("chip", "core")
    placed = (P(rows, "tensor"), P(rows, "tensor"), P("tensor", None), P(rows, None), P(rows))
    return jax.shard_map(
        on_device,
        mesh=fine,
        in_specs=placed,
        out_specs=(P(rows, "tensor"), P(rows, "tensor"), P(rows)),
        check_vma=False,
    )
```

```python
import jax
import jax.numpy as jnp
from jax import lax
from jax.experimental import pallas as pl
from jax.experimental.pallas import tpu as pltpu
from jax.sharding import Mesh
from jax.sharding import PartitionSpec as P

SCALE = 50.0
EPS = 1e-06
WINDOW = 8
CORES = 2
MEMBERS = ("core", "tensor")


def shift_chips(value, by):
    chips = lax.axis_size("chip")
    return lax.ppermute(value, "chip", [(i, (i + by) % chips) for i in range(chips)])


def relay_kernel(value_ref, _, out_ref):
    out_ref[...] = value_ref[...]


def relay(value, wanted, cost):
    return pl.pallas_call(
        relay_kernel,
        in_specs=[pl.BlockSpec(memory_space=pltpu.VMEM), pl.BlockSpec(memory_space=pl.ANY)],
        out_specs=pl.BlockSpec(memory_space=pltpu.VMEM),
        out_shape=jax.ShapeDtypeStruct(value.shape, value.dtype),
        cost_estimate=pl.CostEstimate(flops=cost, bytes_accessed=cost // 1000, transcendentals=0),
    )(value, wanted)


def halves(value, parts):
    out = []
    for _ in range(parts):
        top = lax.reduce_precision(value, 8, 7)
        out.append(top.astype(jnp.bfloat16))
        value = value - top
    return out


def on_device(q_ctx, p_ctx, out_weight, neighbours, positive):
    f32, bf16 = jnp.float32, jnp.bfloat16
    q_rows, p_rows = q_ctx.shape[0], p_ctx.shape[0]
    listed = neighbours.shape[1]
    slots = listed * p_rows
    tensors = lax.axis_size("tensor")
    members = CORES * tensors
    feats = out_weight.shape[1] // members
    q_part = q_rows // tensors
    core, chip = lax.axis_index("core"), lax.axis_index("chip")

    other = lax.ppermute(neighbours, "core", [(0, 1), (1, 0)])
    lists = jnp.concatenate([neighbours, other], axis=0)
    lists = jnp.where(core == 0, lists, lists[::-1])

    def project(rows):
        part = jnp.dot(rows, out_weight, preferred_element_type=f32).astype(bf16)
        return part.reshape(rows.shape[0], members, feats).transpose(1, 0, 2)

    def reduce_over_tensor(part):
        got = lax.all_to_all(part, MEMBERS, 0, 0)
        got = got.reshape(CORES, tensors, part.shape[1], feats).astype(f32)
        return jnp.sum(got, axis=1).astype(bf16)

    p_part = project(p_ctx)
    q_ctx, p_part = lax.optimization_barrier((q_ctx, p_part))
    window = reduce_over_tensor(p_part)
    q_pre = reduce_over_tensor(project(q_ctx))

    reach = 1
    while reach < WINDOW:
        window = jnp.concatenate([window, shift_chips(window, -reach)], axis=0)
        reach *= 2
    spots = (lists - CORES * chip) % (CORES * lax.axis_size("chip"))
    cand = window[spots].reshape(CORES, slots, feats)

    raw = jnp.einsum("kqf,kcf->kqc", q_pre, cand, preferred_element_type=f32)
    q_sq = jnp.sum(jnp.square(q_pre.astype(f32)), axis=-1)
    c_sq = jnp.sum(jnp.square(cand.astype(f32)), axis=-1)
    q_sq = jnp.pad(q_sq.reshape(CORES, tensors, 1, q_part), ((0, 0), (0, 0), (0, 0), (0, slots - q_part)))
    c_sq = jnp.broadcast_to(c_sq[:, None, None, :], (CORES, tensors, 1, slots))
    extra = jnp.zeros((CORES, tensors, 6, slots), f32)
    sums = jnp.concatenate([raw.reshape(CORES, tensors, q_part, slots), q_sq, c_sq, extra], axis=2)
    sums = lax.all_to_all(sums.reshape(members, q_part + 8, slots), MEMBERS, 0, 0)
    sums = jnp.sum(sums, axis=0)
    raw = sums[:q_part]
    inv_q = lax.rsqrt(sums[q_part, :q_part] + EPS)
    inv_c = lax.rsqrt(sums[q_part + 1] + EPS)

    scores = raw * (SCALE * inv_q)[:, None] * inv_c[None, :]
    lse = jnp.log(jnp.sum(jnp.exp(scores), axis=-1))
    pos = lax.dynamic_slice_in_dim(positive, lax.axis_index("tensor") * q_part, q_part)
    onehot = (jnp.arange(slots, dtype=jnp.int32)[None, :] == pos[:, None]).astype(f32)
    loss = lse - jnp.sum(scores * onehot, axis=-1)
    dscore = jnp.exp(scores - lse[:, None]) - onehot
    coef = lax.reduce_precision(dscore * (SCALE * inv_q)[:, None] * inv_c[None, :], 8, 7)
    weighted = coef * raw
    q_inner = jnp.square(inv_q) * jnp.sum(weighted, axis=-1)
    c_inner = jnp.square(inv_c) * jnp.sum(weighted, axis=0)

    row = jnp.concatenate(halves(q_inner, 2) + halves(loss, 3))
    row = jnp.pad(row, (0, slots - row.shape[0]))
    c_rows = jnp.stack([row] + halves(c_inner, 2) + [jnp.zeros((slots,), bf16)] * 5)
    told = jnp.concatenate([coef.astype(bf16), c_rows], axis=0)
    told = lax.all_to_all(jnp.broadcast_to(told[None], (members,) + told.shape), MEMBERS, 0, 0)
    told = told.reshape(CORES, tensors, q_part + 8, slots)
    coef = told[:, :, :q_part].reshape(CORES, q_rows, slots)
    row = told[:, :, q_part].astype(f32)
    q_inner = (row[..., :q_part] + row[..., q_part : 2 * q_part]).reshape(CORES, q_rows, 1)
    loss = row[..., 2 * q_part : 3 * q_part] + row[..., 3 * q_part : 4 * q_part] + row[..., 4 * q_part : 5 * q_part]
    losses = relay(jnp.where(core == 0, loss[0], loss[1]), told, 12500000000).reshape(q_rows)
    c_inner = jnp.sum(told[:, :, q_part + 1 : q_part + 3].astype(f32), axis=(1, 2))[..., None]

    dq = jnp.einsum("kqc,kcf->kqf", coef, cand, preferred_element_type=f32)
    dq = (dq - q_inner * q_pre.astype(f32)).astype(bf16)
    dc = jnp.einsum("kqc,kqf->kcf", coef, q_pre, preferred_element_type=f32)
    dc = (dc - c_inner * cand.astype(f32)).astype(bf16)
    match = (jnp.arange(WINDOW * CORES, dtype=jnp.int32)[:, None, None] == spots[None]).astype(bf16)
    dwin = jnp.einsum("wks,kspf->wpf", match, dc.reshape(CORES, listed, p_rows, feats), preferred_element_type=f32)

    while reach > 1:
        reach //= 2
        away = shift_chips(dwin[CORES * reach :].astype(bf16), reach)
        dwin = dwin[: CORES * reach] + away.astype(f32)
    dp = dwin.astype(bf16)

    def gather_features(part):
        part = jnp.broadcast_to(part[:, None], (CORES, tensors) + part.shape[1:])
        return lax.all_to_all(part.reshape((members,) + part.shape[2:]), MEMBERS, 0, 0)

    def unproject(part):
        weight = out_weight.reshape(out_weight.shape[0], members, feats)
        return jnp.einsum("mrf,hmf->rh", part, weight, preferred_element_type=f32).astype(bf16)

    q_all = gather_features(dq)
    q_all, dp = lax.optimization_barrier((q_all, dp))
    p_grad = unproject(gather_features(dp))
    return unproject(q_all), p_grad, losses


def solution(mesh):
    dp, tensors = mesh.shape["dp"], mesh.shape["tensor"]
    fine = Mesh(mesh.devices.reshape(dp // CORES, CORES, tensors), ("chip", "core", "tensor"))
    rows = ("chip", "core")
    placed = (P(rows, "tensor"), P(rows, "tensor"), P("tensor", None), P(rows, None), P(rows))
    return jax.shard_map(
        on_device,
        mesh=fine,
        in_specs=placed,
        out_specs=(P(rows, "tensor"), P(rows, "tensor"), P(rows)),
        check_vma=False,
    )
```

```python
import jax
import jax.numpy as jnp
from jax import lax
from jax.experimental import pallas as pl
from jax.experimental.pallas import tpu as pltpu
from jax.sharding import Mesh
from jax.sharding import PartitionSpec as P

SCALE = 50.0
EPS = 1e-06
WINDOW = 8
CORES = 2
MEMBERS = ("core", "tensor")


def shift_chips(value, by):
    chips = lax.axis_size("chip")
    return lax.ppermute(value, "chip", [(i, (i + by) % chips) for i in range(chips)])


def relay_kernel(value_ref, _, out_ref):
    out_ref[...] = value_ref[...]


def relay(value, wanted, cost):
    return pl.pallas_call(
        relay_kernel,
        in_specs=[pl.BlockSpec(memory_space=pltpu.VMEM), pl.BlockSpec(memory_space=pl.ANY)],
        out_specs=pl.BlockSpec(memory_space=pltpu.VMEM),
        out_shape=jax.ShapeDtypeStruct(value.shape, value.dtype),
        cost_estimate=pl.CostEstimate(flops=cost, bytes_accessed=cost // 1000, transcendentals=0),
    )(value, wanted)


def once(there, value):
    return jnp.where(there == there, value, jnp.zeros_like(value))


def halves(value, parts):
    out = []
    for _ in range(parts):
        top = lax.reduce_precision(value, 8, 7)
        out.append(top.astype(jnp.bfloat16))
        value = value - top
    return out


def on_device(q_ctx, p_ctx, out_weight, neighbours, positive):
    f32, bf16 = jnp.float32, jnp.bfloat16
    q_rows, p_rows = q_ctx.shape[0], p_ctx.shape[0]
    listed = neighbours.shape[1]
    slots = listed * p_rows
    tensors = lax.axis_size("tensor")
    members = CORES * tensors
    feats = out_weight.shape[1] // members
    q_part = q_rows // tensors
    core, chip = lax.axis_index("core"), lax.axis_index("chip")

    def project(rows):
        part = jnp.dot(rows, out_weight, preferred_element_type=f32).astype(bf16)
        return part.reshape(rows.shape[0], members, feats).transpose(1, 0, 2)

    def reduce_over_tensor(part):
        got = lax.all_to_all(part, MEMBERS, 0, 0)
        got = got.reshape(CORES, tensors, part.shape[1], feats).astype(f32)
        return jnp.sum(got, axis=1).astype(bf16)

    p_part = project(p_ctx)
    q_ctx, p_part = lax.optimization_barrier((q_ctx, p_part))
    window = reduce_over_tensor(p_part)
    q_pre = reduce_over_tensor(project(q_ctx))

    reach = 1
    while reach < WINDOW:
        window = jnp.concatenate([window, shift_chips(window, -reach)], axis=0)
        if reach == 1:
            mine = once(window[-1, 0, 0], neighbours)
            other = lax.ppermute(mine, "core", [(0, 1), (1, 0)])
        reach *= 2
    lists = jnp.concatenate([neighbours, other], axis=0)
    lists = jnp.where(core == 0, lists, lists[::-1])
    spots = (lists - CORES * chip) % (CORES * lax.axis_size("chip"))
    cand = window[spots].reshape(CORES, slots, feats)

    raw = jnp.einsum("kqf,kcf->kqc", q_pre, cand, preferred_element_type=f32)
    q_sq = jnp.sum(jnp.square(q_pre.astype(f32)), axis=-1)
    c_sq = jnp.sum(jnp.square(cand.astype(f32)), axis=-1)
    q_sq = jnp.pad(q_sq.reshape(CORES, tensors, 1, q_part), ((0, 0), (0, 0), (0, 0), (0, slots - q_part)))
    c_sq = jnp.broadcast_to(c_sq[:, None, None, :], (CORES, tensors, 1, slots))
    extra = jnp.zeros((CORES, tensors, 6, slots), f32)
    sums = jnp.concatenate([raw.reshape(CORES, tensors, q_part, slots), q_sq, c_sq, extra], axis=2)
    sums = lax.all_to_all(sums.reshape(members, q_part + 8, slots), MEMBERS, 0, 0)
    sums = jnp.sum(sums, axis=0)
    raw = sums[:q_part]
    inv_q = lax.rsqrt(sums[q_part, :q_part] + EPS)
    inv_c = lax.rsqrt(sums[q_part + 1] + EPS)

    scores = raw * (SCALE * inv_q)[:, None] * inv_c[None, :]
    lse = jnp.log(jnp.sum(jnp.exp(scores), axis=-1))
    pos = lax.dynamic_slice_in_dim(positive, lax.axis_index("tensor") * q_part, q_part)
    onehot = (jnp.arange(slots, dtype=jnp.int32)[None, :] == pos[:, None]).astype(f32)
    loss = lse - jnp.sum(scores * onehot, axis=-1)
    dscore = jnp.exp(scores - lse[:, None]) - onehot
    coef = lax.reduce_precision(dscore * (SCALE * inv_q)[:, None] * inv_c[None, :], 8, 7)
    weighted = coef * raw
    q_inner = jnp.square(inv_q) * jnp.sum(weighted, axis=-1)
    c_inner = jnp.square(inv_c) * jnp.sum(weighted, axis=0)

    row = jnp.concatenate(halves(q_inner, 2) + halves(loss, 3))
    row = jnp.pad(row, (0, slots - row.shape[0]))
    c_rows = jnp.stack([row] + halves(c_inner, 2) + [jnp.zeros((slots,), bf16)] * 5)
    told = jnp.concatenate([coef.astype(bf16), c_rows], axis=0)
    told = lax.all_to_all(jnp.broadcast_to(told[None], (members,) + told.shape), MEMBERS, 0, 0)
    told = told.reshape(CORES, tensors, q_part + 8, slots)
    coef = told[:, :, :q_part].reshape(CORES, q_rows, slots)
    row = told[:, :, q_part].astype(f32)
    q_inner = (row[..., :q_part] + row[..., q_part : 2 * q_part]).reshape(CORES, q_rows, 1)
    loss = row[..., 2 * q_part : 3 * q_part] + row[..., 3 * q_part : 4 * q_part] + row[..., 4 * q_part : 5 * q_part]
    losses = relay(jnp.where(core == 0, loss[0], loss[1]), told, 12500000000).reshape(q_rows)
    c_inner = jnp.sum(told[:, :, q_part + 1 : q_part + 3].astype(f32), axis=(1, 2))[..., None]

    dq = jnp.einsum("kqc,kcf->kqf", coef, cand, preferred_element_type=f32)
    dq = (dq - q_inner * q_pre.astype(f32)).astype(bf16)
    dc = jnp.einsum("kqc,kqf->kcf", coef, q_pre, preferred_element_type=f32)
    dc = (dc - c_inner * cand.astype(f32)).astype(bf16)
    match = (jnp.arange(WINDOW * CORES, dtype=jnp.int32)[:, None, None] == spots[None]).astype(bf16)
    dwin = jnp.einsum("wks,kspf->wpf", match, dc.reshape(CORES, listed, p_rows, feats), preferred_element_type=f32)

    while reach > 1:
        reach //= 2
        away = shift_chips(dwin[CORES * reach :].astype(bf16), reach)
        dwin = dwin[: CORES * reach] + away.astype(f32)
    dp = dwin.astype(bf16)

    def gather_features(part):
        part = jnp.broadcast_to(part[:, None], (CORES, tensors) + part.shape[1:])
        return lax.all_to_all(part.reshape((members,) + part.shape[2:]), MEMBERS, 0, 0)

    def unproject(part):
        weight = out_weight.reshape(out_weight.shape[0], members, feats)
        return jnp.einsum("mrf,hmf->rh", part, weight, preferred_element_type=f32).astype(bf16)

    q_all = gather_features(dq)
    q_all, dp = lax.optimization_barrier((q_all, dp))
    p_grad = unproject(gather_features(dp))
    return unproject(q_all), p_grad, losses


def solution(mesh):
    dp, tensors = mesh.shape["dp"], mesh.shape["tensor"]
    fine = Mesh(mesh.devices.reshape(dp // CORES, CORES, tensors), ("chip", "core", "tensor"))
    rows = ("chip", "core")
    placed = (P(rows, "tensor"), P(rows, "tensor"), P("tensor", None), P(rows, None), P(rows))
    return jax.shard_map(
        on_device,
        mesh=fine,
        in_specs=placed,
        out_specs=(P(rows, "tensor"), P(rows, "tensor"), P(rows)),
        check_vma=False,
    )
```

```python
import jax
import jax.numpy as jnp
from jax import lax
from jax.experimental import pallas as pl
from jax.experimental.pallas import tpu as pltpu
from jax.sharding import Mesh
from jax.sharding import PartitionSpec as P

SCALE = 50.0
EPS = 1e-06
WINDOW = 8
CORES = 2
MEMBERS = ("core", "tensor")


def shift_chips(value, by):
    chips = lax.axis_size("chip")
    return lax.ppermute(value, "chip", [(i, (i + by) % chips) for i in range(chips)])


def relay_kernel(value_ref, _, out_ref):
    out_ref[...] = value_ref[...]


def relay(value, wanted, cost):
    return pl.pallas_call(
        relay_kernel,
        in_specs=[pl.BlockSpec(memory_space=pltpu.VMEM), pl.BlockSpec(memory_space=pl.ANY)],
        out_specs=pl.BlockSpec(memory_space=pltpu.VMEM),
        out_shape=jax.ShapeDtypeStruct(value.shape, value.dtype),
        cost_estimate=pl.CostEstimate(flops=cost, bytes_accessed=cost // 1000, transcendentals=0),
    )(value, wanted)


def halves(value, parts):
    out = []
    for _ in range(parts):
        top = lax.reduce_precision(value, 8, 7)
        out.append(top.astype(jnp.bfloat16))
        value = value - top
    return out


def on_device(q_ctx, p_ctx, out_weight, neighbours, positive):
    f32, bf16 = jnp.float32, jnp.bfloat16
    q_rows, p_rows = q_ctx.shape[0], p_ctx.shape[0]
    listed = neighbours.shape[1]
    slots = listed * p_rows
    tensors = lax.axis_size("tensor")
    members = CORES * tensors
    feats = out_weight.shape[1] // members
    q_part = q_rows // tensors
    core, chip = lax.axis_index("core"), lax.axis_index("chip")

    other = lax.ppermute(neighbours, "core", [(0, 1), (1, 0)])
    lists = jnp.concatenate([neighbours, other], axis=0)
    lists = jnp.where(core == 0, lists, lists[::-1])

    def project(rows):
        part = jnp.dot(rows, out_weight, preferred_element_type=f32).astype(bf16)
        return part.reshape(rows.shape[0], members, feats).transpose(1, 0, 2)

    def reduce_over_tensor(part):
        got = lax.all_to_all(part, MEMBERS, 0, 0)
        got = got.reshape(CORES, tensors, part.shape[1], feats).astype(f32)
        return jnp.sum(got, axis=1).astype(bf16)

    p_part = project(p_ctx)
    q_ctx, p_part = lax.optimization_barrier((q_ctx, p_part))
    window = reduce_over_tensor(p_part)
    q_pre = reduce_over_tensor(project(q_ctx))

    reach = 1
    while reach < WINDOW:
        window = jnp.concatenate([window, shift_chips(window, -reach)], axis=0)
        reach *= 2
    spots = (lists - CORES * chip) % (CORES * lax.axis_size("chip"))
    cand = window[spots].reshape(CORES, slots, feats)

    raw = jnp.einsum("kqf,kcf->kqc", q_pre, cand, preferred_element_type=f32)
    q_sq = jnp.sum(jnp.square(q_pre.astype(f32)), axis=-1)
    c_sq = jnp.sum(jnp.square(cand.astype(f32)), axis=-1)
    q_sq = jnp.pad(q_sq.reshape(CORES, tensors, 1, q_part), ((0, 0), (0, 0), (0, 0), (0, slots - q_part)))
    c_sq = jnp.broadcast_to(c_sq[:, None, None, :], (CORES, tensors, 1, slots))
    extra = jnp.zeros((CORES, tensors, 6, slots), f32)
    sums = jnp.concatenate([raw.reshape(CORES, tensors, q_part, slots), q_sq, c_sq, extra], axis=2)
    sums = lax.all_to_all(sums.reshape(members, q_part + 8, slots), MEMBERS, 0, 0)
    sums = jnp.sum(sums, axis=0)
    raw = sums[:q_part]
    inv_q = lax.rsqrt(sums[q_part, :q_part] + EPS)
    inv_c = lax.rsqrt(sums[q_part + 1] + EPS)

    scores = raw * (SCALE * inv_q)[:, None] * inv_c[None, :]
    lse = jnp.log(jnp.sum(jnp.exp(scores), axis=-1))
    pos = lax.dynamic_slice_in_dim(positive, lax.axis_index("tensor") * q_part, q_part)
    onehot = (jnp.arange(slots, dtype=jnp.int32)[None, :] == pos[:, None]).astype(f32)
    loss = lse - jnp.sum(scores * onehot, axis=-1)
    dscore = jnp.exp(scores - lse[:, None]) - onehot
    coef = lax.reduce_precision(dscore * (SCALE * inv_q)[:, None] * inv_c[None, :], 8, 7)
    weighted = coef * raw
    q_inner = jnp.square(inv_q) * jnp.sum(weighted, axis=-1)
    c_inner = jnp.square(inv_c) * jnp.sum(weighted, axis=0)

    row = jnp.concatenate(halves(q_inner, 2) + halves(loss, 3))
    row = jnp.pad(row, (0, slots - row.shape[0]))
    c_rows = jnp.stack([row] + halves(c_inner, 2) + [jnp.zeros((slots,), bf16)] * 5)
    told = jnp.concatenate([coef.astype(bf16), c_rows], axis=0)
    told = lax.all_to_all(jnp.broadcast_to(told[None], (members,) + told.shape), MEMBERS, 0, 0)
    told = told.reshape(CORES, tensors, q_part + 8, slots)
    coef = told[:, :, :q_part].reshape(CORES, q_rows, slots)
    row = told[:, :, q_part].astype(f32)
    q_inner = (row[..., :q_part] + row[..., q_part : 2 * q_part]).reshape(CORES, q_rows, 1)
    loss = row[..., 2 * q_part : 3 * q_part] + row[..., 3 * q_part : 4 * q_part] + row[..., 4 * q_part : 5 * q_part]
    losses = relay(jnp.where(core == 0, loss[0], loss[1]), told, 12500000000).reshape(q_rows)
    c_inner = jnp.sum(told[:, :, q_part + 1 : q_part + 3].astype(f32), axis=(1, 2))[..., None]

    dq = jnp.einsum("kqc,kcf->kqf", coef, cand, preferred_element_type=f32)
    dq = (dq - q_inner * q_pre.astype(f32)).astype(bf16)
    dc = jnp.einsum("kqc,kqf->kcf", coef, q_pre, preferred_element_type=f32)
    dc = (dc - c_inner * cand.astype(f32)).astype(bf16)
    far = spots // CORES
    slot = (far % 2 * 4 + far // 2 % 2 * 2 + far // 4) * CORES + spots % CORES
    match = (jnp.arange(WINDOW * CORES, dtype=jnp.int32)[:, None, None] == slot[None]).astype(bf16)
    dwin = jnp.einsum("wks,kspf->wpf", match, dc.reshape(CORES, listed, p_rows, feats), preferred_element_type=f32)

    reach = 1
    while reach < WINDOW:
        half = dwin.shape[0] // 2
        dwin = dwin[:half] + shift_chips(dwin[half:].astype(bf16), reach).astype(f32)
        reach *= 2
    dp = dwin.astype(bf16)

    def copies(part):
        part = jnp.broadcast_to(part[:, None], (CORES, tensors) + part.shape[1:])
        return part.reshape((members,) + part.shape[2:])

    def unproject(part):
        weight = out_weight.reshape(out_weight.shape[0], members, feats)
        return jnp.einsum("mrf,hmf->rh", part, weight, preferred_element_type=f32).astype(bf16)

    q_all = lax.all_to_all(copies(dq), MEMBERS, 0, 0)
    q_all, dp = lax.optimization_barrier((q_all, copies(dp)))
    p_grad = unproject(lax.all_to_all(dp, MEMBERS, 0, 0))
    return unproject(q_all), p_grad, losses


def solution(mesh):
    dp, tensors = mesh.shape["dp"], mesh.shape["tensor"]
    fine = Mesh(mesh.devices.reshape(dp // CORES, CORES, tensors), ("chip", "core", "tensor"))
    rows = ("chip", "core")
    placed = (P(rows, "tensor"), P(rows, "tensor"), P("tensor", None), P(rows, None), P(rows))
    return jax.shard_map(
        on_device,
        mesh=fine,
        in_specs=placed,
        out_specs=(P(rows, "tensor"), P(rows, "tensor"), P(rows)),
        check_vma=False,
    )
```

```python
import jax
import jax.numpy as jnp
from jax import lax
from jax.experimental import pallas as pl
from jax.experimental.pallas import tpu as pltpu
from jax.sharding import Mesh
from jax.sharding import PartitionSpec as P

SCALE = 50.0
EPS = 1e-06
WINDOW = 8
CORES = 2
MEMBERS = ("core", "tensor")


def shift_chips(value, by):
    chips = lax.axis_size("chip")
    return lax.ppermute(value, "chip", [(i, (i + by) % chips) for i in range(chips)])


def relay_kernel(value_ref, _, out_ref):
    out_ref[...] = value_ref[...]


def relay(value, wanted, cost):
    return pl.pallas_call(
        relay_kernel,
        in_specs=[pl.BlockSpec(memory_space=pltpu.VMEM), pl.BlockSpec(memory_space=pl.ANY)],
        out_specs=pl.BlockSpec(memory_space=pltpu.VMEM),
        out_shape=jax.ShapeDtypeStruct(value.shape, value.dtype),
        cost_estimate=pl.CostEstimate(flops=cost, bytes_accessed=cost // 1000, transcendentals=0),
    )(value, wanted)


def halves(value, parts):
    out = []
    for _ in range(parts):
        top = lax.reduce_precision(value, 8, 7)
        out.append(top.astype(jnp.bfloat16))
        value = value - top
    return out


def unproject_kernel(x_ref, w_ref, out_ref, sum_ref):
    step = pl.program_id(0)
    per, _, feats = x_ref.shape

    @pl.when(step == 0)
    def _():
        sum_ref[...] = jnp.zeros_like(sum_ref)

    total = sum_ref[...]
    for j in range(per):
        total += lax.dot_general(
            w_ref[:, j * feats : (j + 1) * feats],
            x_ref[j],
            (((1,), (1,)), ((), ())),
            preferred_element_type=jnp.float32,
        )
    sum_ref[...] = total

    @pl.when(step == pl.num_programs(0) - 1)
    def _():
        out_ref[...] = total.T.astype(out_ref.dtype)


def unproject_few(part, weight, steps=4):
    members, rows, feats = part.shape
    depth, width = weight.shape
    return pl.pallas_call(
        unproject_kernel,
        grid=(steps,),
        in_specs=[
            pl.BlockSpec((members // steps, rows, feats), lambda g: (g, 0, 0)),
            pl.BlockSpec((depth, width // steps), lambda g: (0, g)),
        ],
        out_specs=pl.BlockSpec((rows, depth), lambda g: (0, 0)),
        out_shape=jax.ShapeDtypeStruct((rows, depth), jnp.bfloat16),
        scratch_shapes=[pltpu.VMEM((depth, rows), jnp.float32)],
        cost_estimate=pl.CostEstimate(
            flops=2 * rows * depth * width, bytes_accessed=2 * depth * width, transcendentals=0
        ),
    )(part, weight)


def on_device(q_ctx, p_ctx, out_weight, neighbours, positive):
    f32, bf16 = jnp.float32, jnp.bfloat16
    q_rows, p_rows = q_ctx.shape[0], p_ctx.shape[0]
    listed = neighbours.shape[1]
    slots = listed * p_rows
    tensors = lax.axis_size("tensor")
    members = CORES * tensors
    feats = out_weight.shape[1] // members
    q_part = q_rows // tensors
    core, chip = lax.axis_index("core"), lax.axis_index("chip")

    other = lax.ppermute(neighbours, "core", [(0, 1), (1, 0)])
    lists = jnp.concatenate([neighbours, other], axis=0)
    lists = jnp.where(core == 0, lists, lists[::-1])

    def project(rows):
        part = jnp.dot(rows, out_weight, preferred_element_type=f32).astype(bf16)
        return part.reshape(rows.shape[0], members, feats).transpose(1, 0, 2)

    def reduce_over_tensor(part):
        got = lax.all_to_all(part, MEMBERS, 0, 0)
        got = got.reshape(CORES, tensors, part.shape[1], feats).astype(f32)
        return jnp.sum(got, axis=1).astype(bf16)

    p_part = project(p_ctx)
    q_ctx, p_part = lax.optimization_barrier((q_ctx, p_part))
    window = reduce_over_tensor(p_part)
    q_pre = reduce_over_tensor(project(q_ctx))

    reach = 1
    while reach < WINDOW:
        window = jnp.concatenate([window, shift_chips(window, -reach)], axis=0)
        reach *= 2
    spots = (lists - CORES * chip) % (CORES * lax.axis_size("chip"))
    cand = window[spots].reshape(CORES, slots, feats)

    raw = jnp.einsum("kqf,kcf->kqc", q_pre, cand, preferred_element_type=f32)
    q_sq = jnp.sum(jnp.square(q_pre.astype(f32)), axis=-1)
    c_sq = jnp.sum(jnp.square(cand.astype(f32)), axis=-1)
    q_sq = jnp.pad(q_sq.reshape(CORES, tensors, 1, q_part), ((0, 0), (0, 0), (0, 0), (0, slots - q_part)))
    c_sq = jnp.broadcast_to(c_sq[:, None, None, :], (CORES, tensors, 1, slots))
    extra = jnp.zeros((CORES, tensors, 6, slots), f32)
    sums = jnp.concatenate([raw.reshape(CORES, tensors, q_part, slots), q_sq, c_sq, extra], axis=2)
    sums = lax.all_to_all(sums.reshape(members, q_part + 8, slots), MEMBERS, 0, 0)
    sums = jnp.sum(sums, axis=0)
    raw = sums[:q_part]
    inv_q = lax.rsqrt(sums[q_part, :q_part] + EPS)
    inv_c = lax.rsqrt(sums[q_part + 1] + EPS)

    scores = raw * (SCALE * inv_q)[:, None] * inv_c[None, :]
    lse = jnp.log(jnp.sum(jnp.exp(scores), axis=-1))
    pos = lax.dynamic_slice_in_dim(positive, lax.axis_index("tensor") * q_part, q_part)
    onehot = (jnp.arange(slots, dtype=jnp.int32)[None, :] == pos[:, None]).astype(f32)
    loss = lse - jnp.sum(scores * onehot, axis=-1)
    dscore = jnp.exp(scores - lse[:, None]) - onehot
    coef = lax.reduce_precision(dscore * (SCALE * inv_q)[:, None] * inv_c[None, :], 8, 7)
    weighted = coef * raw
    q_inner = jnp.square(inv_q) * jnp.sum(weighted, axis=-1)
    c_inner = jnp.square(inv_c) * jnp.sum(weighted, axis=0)

    row = jnp.concatenate(halves(q_inner, 2) + halves(loss, 3))
    row = jnp.pad(row, (0, slots - row.shape[0]))
    c_rows = jnp.stack([row] + halves(c_inner, 2) + [jnp.zeros((slots,), bf16)] * 5)
    told = jnp.concatenate([coef.astype(bf16), c_rows], axis=0)
    told = lax.all_to_all(jnp.broadcast_to(told[None], (members,) + told.shape), MEMBERS, 0, 0)
    told = told.reshape(CORES, tensors, q_part + 8, slots)
    coef = told[:, :, :q_part].reshape(CORES, q_rows, slots)
    row = told[:, :, q_part].astype(f32)
    q_inner = (row[..., :q_part] + row[..., q_part : 2 * q_part]).reshape(CORES, q_rows, 1)
    loss = row[..., 2 * q_part : 3 * q_part] + row[..., 3 * q_part : 4 * q_part] + row[..., 4 * q_part : 5 * q_part]
    losses = relay(jnp.where(core == 0, loss[0], loss[1]), told, 12500000000).reshape(q_rows)
    c_inner = jnp.sum(told[:, :, q_part + 1 : q_part + 3].astype(f32), axis=(1, 2))[..., None]

    dq = jnp.einsum("kqc,kcf->kqf", coef, cand, preferred_element_type=f32)
    dq = (dq - q_inner * q_pre.astype(f32)).astype(bf16)
    dc = jnp.einsum("kqc,kqf->kcf", coef, q_pre, preferred_element_type=f32)
    dc = (dc - c_inner * cand.astype(f32)).astype(bf16)
    match = (jnp.arange(WINDOW * CORES, dtype=jnp.int32)[:, None, None] == spots[None]).astype(bf16)
    dwin = jnp.einsum("wks,kspf->wpf", match, dc.reshape(CORES, listed, p_rows, feats), preferred_element_type=f32)

    while reach > 1:
        reach //= 2
        away = shift_chips(dwin[CORES * reach :].astype(bf16), reach)
        dwin = dwin[: CORES * reach] + away.astype(f32)
    dp = dwin.astype(bf16)

    def gather_features(part):
        part = jnp.broadcast_to(part[:, None], (CORES, tensors) + part.shape[1:])
        return lax.all_to_all(part.reshape((members,) + part.shape[2:]), MEMBERS, 0, 0)

    def unproject(part):
        weight = out_weight.reshape(out_weight.shape[0], members, feats)
        return jnp.einsum("mrf,hmf->rh", part, weight, preferred_element_type=f32).astype(bf16)

    q_all = gather_features(dq)
    q_all, dp = lax.optimization_barrier((q_all, dp))
    p_grad = unproject_few(gather_features(dp), out_weight)
    return unproject(q_all), p_grad, losses


def solution(mesh):
    dp, tensors = mesh.shape["dp"], mesh.shape["tensor"]
    fine = Mesh(mesh.devices.reshape(dp // CORES, CORES, tensors), ("chip", "core", "tensor"))
    rows = ("chip", "core")
    placed = (P(rows, "tensor"), P(rows, "tensor"), P("tensor", None), P(rows, None), P(rows))
    return jax.shard_map(
        on_device,
        mesh=fine,
        in_specs=placed,
        out_specs=(P(rows, "tensor"), P(rows, "tensor"), P(rows)),
        check_vma=False,
    )
```

```python
import jax
import jax.numpy as jnp
from jax import lax
from jax.experimental import pallas as pl
from jax.experimental.pallas import tpu as pltpu
from jax.sharding import Mesh
from jax.sharding import PartitionSpec as P

SCALE = 50.0
EPS = 1e-06
WINDOW = 8
CORES = 2
MEMBERS = ("core", "tensor")


def shift_chips(value, by):
    chips = lax.axis_size("chip")
    return lax.ppermute(value, "chip", [(i, (i + by) % chips) for i in range(chips)])


def relay_kernel(value_ref, _, out_ref):
    out_ref[...] = value_ref[...]


def relay(value, wanted, cost):
    return pl.pallas_call(
        relay_kernel,
        in_specs=[pl.BlockSpec(memory_space=pltpu.VMEM), pl.BlockSpec(memory_space=pl.ANY)],
        out_specs=pl.BlockSpec(memory_space=pltpu.VMEM),
        out_shape=jax.ShapeDtypeStruct(value.shape, value.dtype),
        cost_estimate=pl.CostEstimate(flops=cost, bytes_accessed=cost // 1000, transcendentals=0),
    )(value, wanted)


def halves(value, parts):
    out = []
    for _ in range(parts):
        top = lax.reduce_precision(value, 8, 7)
        out.append(top.astype(jnp.bfloat16))
        value = value - top
    return out


def on_device(q_ctx, p_ctx, out_weight, neighbours, positive):
    f32, bf16 = jnp.float32, jnp.bfloat16
    q_rows, p_rows = q_ctx.shape[0], p_ctx.shape[0]
    listed = neighbours.shape[1]
    slots = listed * p_rows
    tensors = lax.axis_size("tensor")
    members = CORES * tensors
    feats = out_weight.shape[1] // members
    q_part = q_rows // tensors
    core, chip = lax.axis_index("core"), lax.axis_index("chip")

    other = lax.ppermute(neighbours, "core", [(0, 1), (1, 0)])
    lists = jnp.concatenate([neighbours, other], axis=0)
    lists = jnp.where(core == 0, lists, lists[::-1])

    def project(rows):
        part = jnp.dot(rows, out_weight, preferred_element_type=f32).astype(bf16)
        return part.reshape(rows.shape[0], members, feats).transpose(1, 0, 2)

    def reduce_over_tensor(part):
        got = lax.all_to_all(part, MEMBERS, 0, 0)
        got = got.reshape(CORES, tensors, part.shape[1], feats).astype(f32)
        return jnp.sum(got, axis=1).astype(bf16)

    p_part = project(p_ctx)
    q_ctx, p_part = lax.optimization_barrier((q_ctx, p_part))
    window = reduce_over_tensor(p_part)
    q_pre = reduce_over_tensor(project(q_ctx))

    reach = 1
    while reach < WINDOW:
        window = jnp.concatenate([window, shift_chips(window, -reach)], axis=0)
        reach *= 2
    spots = (lists - CORES * chip) % (CORES * lax.axis_size("chip"))
    cand = window[spots].reshape(CORES, slots, feats)

    raw = jnp.einsum("kqf,kcf->kqc", q_pre, cand, preferred_element_type=f32)
    q_sq = jnp.sum(jnp.square(q_pre.astype(f32)), axis=-1)
    c_sq = jnp.sum(jnp.square(cand.astype(f32)), axis=-1)
    q_sq = jnp.pad(q_sq.reshape(CORES, tensors, 1, q_part), ((0, 0), (0, 0), (0, 0), (0, slots - q_part)))
    c_sq = jnp.broadcast_to(c_sq[:, None, None, :], (CORES, tensors, 1, slots))
    extra = jnp.zeros((CORES, tensors, 6, slots), f32)
    sums = jnp.concatenate([raw.reshape(CORES, tensors, q_part, slots), q_sq, c_sq, extra], axis=2)
    sums = lax.all_to_all(sums.reshape(members, q_part + 8, slots), MEMBERS, 0, 0)
    sums = jnp.sum(sums, axis=0)
    raw = sums[:q_part]
    inv_q = lax.rsqrt(sums[q_part, :q_part] + EPS)
    inv_c = lax.rsqrt(sums[q_part + 1] + EPS)

    scores = raw * (SCALE * inv_q)[:, None] * inv_c[None, :]
    lse = jnp.log(jnp.sum(jnp.exp(scores), axis=-1))
    pos = lax.dynamic_slice_in_dim(positive, lax.axis_index("tensor") * q_part, q_part)
    onehot = (jnp.arange(slots, dtype=jnp.int32)[None, :] == pos[:, None]).astype(f32)
    loss = lse - jnp.sum(scores * onehot, axis=-1)
    dscore = jnp.exp(scores - lse[:, None]) - onehot
    coef = lax.reduce_precision(dscore * (SCALE * inv_q)[:, None] * inv_c[None, :], 8, 7)
    weighted = coef * raw
    q_inner = jnp.square(inv_q) * jnp.sum(weighted, axis=-1)
    c_inner = jnp.square(inv_c) * jnp.sum(weighted, axis=0)

    row = jnp.concatenate(halves(q_inner, 2) + halves(loss, 3))
    row = jnp.pad(row, (0, slots - row.shape[0]))
    c_rows = jnp.stack([row] + halves(c_inner, 2) + [jnp.zeros((slots,), bf16)] * 5)
    told = jnp.concatenate([coef.astype(bf16), c_rows], axis=0)
    told = lax.all_to_all(jnp.broadcast_to(told[None], (members,) + told.shape), MEMBERS, 0, 0)
    told = told.reshape(CORES, tensors, q_part + 8, slots)
    coef = told[:, :, :q_part].reshape(CORES, q_rows, slots)
    row = told[:, :, q_part].astype(f32)
    q_inner = (row[..., :q_part] + row[..., q_part : 2 * q_part]).reshape(CORES, q_rows, 1)
    loss = row[..., 2 * q_part : 3 * q_part] + row[..., 3 * q_part : 4 * q_part] + row[..., 4 * q_part : 5 * q_part]
    losses = relay(jnp.where(core == 0, loss[0], loss[1]), told, 12500000000).reshape(q_rows)
    c_inner = jnp.sum(told[:, :, q_part + 1 : q_part + 3].astype(f32), axis=(1, 2))[..., None]

    dq = jnp.einsum("kqc,kcf->kqf", coef, cand, preferred_element_type=f32)
    dq = (dq - q_inner * q_pre.astype(f32)).astype(bf16)
    dc = jnp.einsum("kqc,kqf->kcf", coef, q_pre, preferred_element_type=f32)
    dc = (dc - c_inner * cand.astype(f32)).astype(bf16)
    far = spots // CORES
    slot = (far // 4 * 4 + far % 2 * 2 + far // 2 % 2) * CORES + spots % CORES
    match = (jnp.arange(WINDOW * CORES, dtype=jnp.int32)[:, None, None] == slot[None]).astype(bf16)
    dwin = jnp.einsum("wks,kspf->wpf", match, dc.reshape(CORES, listed, p_rows, feats), preferred_element_type=f32)

    for by in (4, 1, 2):
        half = dwin.shape[0] // 2
        dwin = dwin[:half] + shift_chips(dwin[half:].astype(bf16), by).astype(f32)
    dp = dwin.astype(bf16)

    def gather_features(part):
        part = jnp.broadcast_to(part[:, None], (CORES, tensors) + part.shape[1:])
        return lax.all_to_all(part.reshape((members,) + part.shape[2:]), MEMBERS, 0, 0)

    def unproject(part):
        weight = out_weight.reshape(out_weight.shape[0], members, feats)
        return jnp.einsum("mrf,hmf->rh", part, weight, preferred_element_type=f32).astype(bf16)

    q_all = gather_features(dq)
    q_all, dp = lax.optimization_barrier((q_all, dp))
    p_grad = unproject(gather_features(dp))
    return unproject(q_all), p_grad, losses


def solution(mesh):
    dp, tensors = mesh.shape["dp"], mesh.shape["tensor"]
    fine = Mesh(mesh.devices.reshape(dp // CORES, CORES, tensors), ("chip", "core", "tensor"))
    rows = ("chip", "core")
    placed = (P(rows, "tensor"), P(rows, "tensor"), P("tensor", None), P(rows, None), P(rows))
    return jax.shard_map(
        on_device,
        mesh=fine,
        in_specs=placed,
        out_specs=(P(rows, "tensor"), P(rows, "tensor"), P(rows)),
        check_vma=False,
    )
```
